128 devices in a mesh: pair: 32 (over x, z_hi, y), row: 4 (over z_lo, core).
Axes of the slice: x: 4, y: 4, z: 4 (z_hi: 2, z_lo: 2; z = z_hi * 2 + z_lo), core: 2. Of those that a mesh axis runs over, the one named last changes fastest.
Arguments:
- weight: bfloat16 [8192, 32768], P(('pair', 'row')), may hold values from -24 to 24
Outputs:
- rotated: bfloat16 [8192, 32768], P(('pair', 'row'))
The draws below stay inside these ranges and needn't reach their ends.
All inputs are finite; a program needn't handle non-finite values.
Results may differ from the reference program's by a relative error of at most 0.0082.
Values may be sent and summed in bfloat16 or wider, within the bound.
No kernel may reach another device: no remote copies, remote signals or barrier semaphores. Data moves between devices by JAX's collectives and lax.ppermute only.
A program may use at most 128 MiB of HBM per device.

```python
import math
import jax
import jax.numpy as jnp
from jax import lax

ROWS = 8192
BLK = 512
ROUNDS = 2
COLS = 32768
N_PAIR = 32


def draw_weight(key, part):
    key_z, key_shared, key_mix, key_cols = jax.random.split(key, 4)
    noise = jax.random.normal(key_z, (ROWS, COLS), jnp.float32)
    row_scales = jnp.ones((ROWS, 1), jnp.float32)
    shared = jax.random.normal(key_shared, (ROWS, 16), jnp.float32)
    mixing = jax.random.normal(key_mix, (COLS,), jnp.float32)
    col_scales = jnp.exp(jax.random.uniform(key_cols, (COLS,), jnp.float32, math.log(0.4), math.log(4.0)))
    values = row_scales * col_scales[None, :] * (noise + 0.3 * mixing[None, :] * jnp.tile(shared, (1, COLS // 16)))
    return jnp.clip(values, -24.0, 24.0).astype(jnp.bfloat16)


def setup_inputs(seed: int = 0) -> dict:
    key_list = jax.random.split(jax.random.key(seed), 2)
    weight = draw_weight(jax.random.fold_in(key_list[1], 71), 0)
    return dict(weight=weight)


def inner_cols(left_cols, right_cols):
    return lax.dot_general(left_cols, right_cols, (((0,), (0,)), ((), ())), precision=lax.Precision.HIGHEST, preferred_element_type=jnp.float32)

def rotation_from(gram_sum):
    width = gram_sum.shape[0]
    identity = jnp.eye(width, dtype=jnp.float32)
    diag_vals = jnp.diagonal(gram_sum)
    upper = jnp.triu(gram_sum, 1) / (diag_vals[:, None] + diag_vals[None, :] + 0.001)
    generator = upper - upper.T
    norm_sq = 1.0 + jnp.sum(generator * generator) / width
    inv_norm = lax.rsqrt(norm_sq)
    gen_low = generator.astype(jnp.bfloat16)
    squared = jnp.dot(gen_low, gen_low, preferred_element_type=jnp.float32)
    middle = (1.5 * identity - 0.5 * inv_norm * inv_norm * (identity - squared)).astype(jnp.bfloat16)
    start_rot = ((identity + generator) * inv_norm).astype(jnp.bfloat16)
    return jnp.dot(start_rot, middle, preferred_element_type=jnp.float32).astype(jnp.bfloat16)

def rotate_pair(block):
    wide = block.astype(jnp.float32)
    rotation = rotation_from(inner_cols(wide, wide))
    return jnp.dot(wide, rotation.astype(jnp.float32), precision=lax.Precision.HIGHEST, preferred_element_type=jnp.float32).astype(jnp.bfloat16)

def reference(weight):
    blocks = weight.reshape(ROWS, N_PAIR, 2 * BLK).transpose(1, 0, 2)
    for round_no in range(ROUNDS):
        blocks = lax.map(rotate_pair, blocks)
        if round_no < ROUNDS - 1:
            upper_half = blocks[:, :, :BLK]
            lower_half = blocks[:, :, BLK:]
            new_upper = jnp.concatenate([upper_half[:1], lower_half[:1], upper_half[1:N_PAIR - 1]], axis=0)
            new_lower = jnp.concatenate([lower_half[1:], upper_half[N_PAIR - 1:]], axis=0)
            blocks = jnp.concatenate([new_upper, new_lower], axis=2)
    return blocks.transpose(1, 0, 2).reshape(ROWS, COLS)
```

```python
import jax
import jax.numpy as jnp
import numpy as np
from jax import lax
from jax.experimental import pallas as pl
from jax.experimental.pallas import tpu as pltpu
from jax.sharding import Mesh
from jax.sharding import PartitionSpec as P

NODES = 32
HALF = 512
WIDE = 1024
TILE = 256
PER = 64
ROWS = NODES * PER
AXES = ("x", "zh", "y", "zl", "core")
NODE_AXES = ("x", "y", "zl")
F32 = jnp.float32
BF16 = jnp.bfloat16
VMEM = pl.BlockSpec(memory_space=pltpu.VMEM)
SMEM = pl.BlockSpec(memory_space=pltpu.SMEM)
HBM = pl.BlockSpec(memory_space=pl.ANY)

RING = [0] + list(range(1, 32, 2)) + list(range(30, 0, -2))


def ring_places():
    plane = []
    for x in range(4):
        ys = range(4) if x % 2 == 0 else range(3, -1, -1)
        plane += [(x, y) for y in ys]
    low = [x * 8 + y * 2 for x, y in plane]
    high = [x * 8 + y * 2 + 1 for x, y in plane[::-1]]
    return low + high


PLACE = ring_places()
NODE_AT = [PLACE.index(n) for n in range(NODES)]


def edge_pair(edge):
    return 2 * edge if edge <= 15 else 63 - 2 * edge


def flat(place, zh, core):
    x, y, zl = place // 8, place // 2 % 4, place % 2
    return (((x * 2 + zh) * 4 + y) * 2 + zl) * 2 + core


def all_perm(target):
    return [
        (flat(PLACE[j], zh, c), flat(*target(j, zh, c)))
        for j in range(NODES)
        for zh in range(2)
        for c in range(2)
    ]


CORE_SWAP = all_perm(lambda j, zh, c: (PLACE[j], zh, 1 - c))
Z_SWAP = all_perm(lambda j, zh, c: (PLACE[j], 1 - zh, c))
RING_SEND = all_perm(lambda j, zh, c: (PLACE[(j + 1 - 2 * c) % NODES], zh, c))
CHAIN_SWAP = all_perm(lambda j, zh, c: (PLACE[(j - 1 + 2 * c) % NODES], zh, 1 - c))


def permute(value, table):
    return lax.ppermute(value, AXES, table)


def params(mebibytes=40):
    return pltpu.CompilerParams(vmem_limit_bytes=mebibytes * 1024 * 1024)


def cost(macs, nbytes):
    return pl.CostEstimate(flops=2 * macs, bytes_accessed=nbytes, transcendentals=0)


def struct(shape, dtype):
    return jax.ShapeDtypeStruct(shape, dtype)


def gram_dot(left, right):
    return lax.dot_general(left, right, (((0,), (0,)), ((), ())), preferred_element_type=F32)


GROUP = 4
STAGE = [pltpu.SemaphoreType.DMA((NODES,)), pltpu.SemaphoreType.DMA((NODES // GROUP,))]


def run_stages(loads, stores):
    for load in loads:
        load.start()
    for k, store in enumerate(stores):
        for load in loads[GROUP * k : GROUP * (k + 1)]:
            load.wait()
        store.start()
    for store in stores:
        store.wait()


def spread_kernel(weight_ref, out_ref, held, load_sems, store_sems):
    loads = [
        pltpu.make_async_copy(
            weight_ref.at[:, pl.ds(RING[NODE_AT[n]] * WIDE, WIDE)], held.at[n], load_sems.at[n]
        )
        for n in range(NODES)
    ]
    stores = [
        pltpu.make_async_copy(
            held.at[pl.ds(k * GROUP, GROUP)], out_ref.at[pl.ds(k * GROUP, GROUP)], store_sems.at[k]
        )
        for k in range(NODES // GROUP)
    ]
    run_stages(loads, stores)


def spread(weight):
    return pl.pallas_call(
        spread_kernel,
        out_shape=struct((NODES, PER, WIDE), BF16),
        in_specs=[HBM],
        out_specs=HBM,
        scratch_shapes=[pltpu.VMEM((NODES, PER, WIDE), BF16)] + STAGE,
        compiler_params=params(60),
        cost_estimate=cost(0, 2 * ROWS * WIDE * 2),
        name="spread",
    )(weight)


def gather_kernel(source_ref, parts_ref, out_ref, held, load_sems, store_sems):
    loads = [
        pltpu.make_async_copy(
            parts_ref.at[source_ref[q]], held.at[:, pl.ds(q * WIDE, WIDE)], load_sems.at[q]
        )
        for q in range(NODES)
    ]
    span = GROUP * WIDE
    stores = [
        pltpu.make_async_copy(
            held.at[:, pl.ds(k * span, span)], out_ref.at[:, pl.ds(k * span, span)], store_sems.at[k]
        )
        for k in range(NODES // GROUP)
    ]
    run_stages(loads, stores)


def gather(parts, source):
    return pl.pallas_call(
        gather_kernel,
        out_shape=struct((PER, NODES * WIDE), BF16),
        in_specs=[SMEM, HBM],
        out_specs=HBM,
        scratch_shapes=[pltpu.VMEM((PER, NODES * WIDE), BF16)] + STAGE,
        compiler_params=params(60),
        cost_estimate=cost(0, 2 * ROWS * WIDE * 2),
        name="gather",
    )(source, parts)


TILES = [(0, 0), (0, 1), (1, 1), (0, 2), (0, 3), (2, 2), (2, 3), (3, 3), (1, 2), (1, 3)]
DIAG_TILES = [(0, 0), (0, 1), (1, 1)]


def gram_kernel(core_ref, cols_ref, mine_ref, other_ref):
    core = core_ref[0]
    for row in range(4):
        strip = gram_dot(cols_ref[:, row * TILE : (row + 1) * TILE], cols_ref[:, row * TILE :])
        for col in range(row, 4):
            tile = strip[:, (col - row) * TILE : (col - row + 1) * TILE]
            place = TILES.index((row, col))
            owner, slot = divmod(place, 5)

            @pl.when(core == owner)
            def _():
                mine_ref[slot] = tile

            @pl.when(core != owner)
            def _():
                other_ref[slot] = tile.astype(BF16)


def gram(core, cols):
    return pl.pallas_call(
        gram_kernel,
        out_shape=(struct((5, TILE, TILE), F32), struct((5, TILE, TILE), BF16)),
        in_specs=[SMEM, VMEM],
        out_specs=(VMEM, VMEM),
        compiler_params=params(),
        cost_estimate=cost(10 * ROWS * TILE * TILE, ROWS * WIDE * 2 + 2**21),
        name="gram",
    )(core, cols)


def rotation_body(tiles, sign, rot_ref, gen, gen_low, middle):
    rows = lax.broadcasted_iota(jnp.int32, (TILE, TILE), 0)
    cols = lax.broadcasted_iota(jnp.int32, (TILE, TILE), 1)
    down, across = [], []
    for i in range(4):
        only = jnp.where(rows == cols, tiles(i, i), 0.0)
        down.append(jnp.sum(only, axis=1, keepdims=True))
        across.append(jnp.sum(only, axis=0, keepdims=True))
    total = jnp.zeros((TILE, TILE), F32)
    for i in range(4):
        for j in range(i, 4):
            upper = tiles(i, j) / (down[i] + across[j] + 0.001)
            if i == j:
                upper = jnp.where(rows < cols, upper, 0.0)
            elif i < 2 <= j and sign is not None:
                upper = upper * sign
            total = total + upper * upper
            at_i, at_j = pl.ds(i * TILE, TILE), pl.ds(j * TILE, TILE)
            if i == j:
                both = upper - upper.T
                gen[at_i, at_j] = both
                gen_low[at_i, at_j] = both.astype(BF16)
            else:
                flipped = -upper.T
                gen[at_i, at_j] = upper
                gen_low[at_i, at_j] = upper.astype(BF16)
                gen[at_j, at_i] = flipped
                gen_low[at_j, at_i] = flipped.astype(BF16)
    norm_sq = 1.0 + 2.0 * jnp.sum(total, keepdims=True) / WIDE
    inv_norm = lax.rsqrt(norm_sq)
    scale = 0.5 * inv_norm * inv_norm
    wide_rows = lax.broadcasted_iota(jnp.int32, (TILE, WIDE), 0)
    wide_cols = lax.broadcasted_iota(jnp.int32, (TILE, WIDE), 1)
    for i in range(4):
        at = pl.ds(i * TILE, TILE)
        squared = jnp.dot(gen_low[at, :], gen_low[...], preferred_element_type=F32)
        identity = jnp.where(wide_rows + i * TILE == wide_cols, 1.0, 0.0)
        middle[at, :] = (1.5 * identity - scale * (identity - squared)).astype(BF16)
    for i in range(4):
        at = pl.ds(i * TILE, TILE)
        identity = jnp.where(wide_rows + i * TILE == wide_cols, 1.0, 0.0)
        start_rot = ((identity + gen[at, :]) * inv_norm).astype(BF16)
        rot_ref[at, :] = jnp.dot(start_rot, middle[...], preferred_element_type=F32).astype(BF16)


ROTATION_SCRATCH = [
    pltpu.VMEM((WIDE, WIDE), F32),
    pltpu.VMEM((WIDE, WIDE), BF16),
    pltpu.VMEM((WIDE, WIDE), BF16),
]


def rotation_one_kernel(core_ref, own_ref, far_ref, rot_ref, gen, gen_low, middle, held):
    core = core_ref[0]
    held[core] = own_ref[...]
    held[1 - core] = far_ref[...]

    def tiles(i, j):
        owner, slot = divmod(TILES.index((i, j)), 5)
        return held[owner, slot].astype(F32)

    rotation_body(tiles, None, rot_ref, gen, gen_low, middle)


def rotation_one(core, own, far):
    return pl.pallas_call(
        rotation_one_kernel,
        out_shape=struct((WIDE, WIDE), BF16),
        in_specs=[SMEM, VMEM, VMEM],
        out_specs=VMEM,
        scratch_shapes=ROTATION_SCRATCH + [pltpu.VMEM((2, 5, TILE, TILE), BF16)],
        compiler_params=params(),
        cost_estimate=cost(2 * WIDE**3, 4 * 2**20),
        name="rotation_one",
    )(core, own, far)


def rotation_two_kernel(
    flags_ref, recv_ref, keep_ref, top_ref, low_ref, rot_ref, gen, gen_low, middle, held
):
    first = flags_ref[0]
    sign = jnp.where(flags_ref[1] == 1, 1.0, -1.0)
    held[first] = recv_ref[...]
    held[1 - first] = keep_ref[...]

    def tiles(i, j):
        if i < 2 <= j:
            half = top_ref if i == 0 else low_ref
            return half[:, (j - 2) * TILE : (j - 1) * TILE].astype(F32)
        block = i // 2
        return held[block, DIAG_TILES.index((i - 2 * block, j - 2 * block))].astype(F32)

    rotation_body(tiles, sign, rot_ref, gen, gen_low, middle)


def rotation_two(flags, recv_diag, keep_diag, top, low):
    return pl.pallas_call(
        rotation_two_kernel,
        out_shape=struct((WIDE, WIDE), BF16),
        in_specs=[SMEM] + [VMEM] * 4,
        out_specs=VMEM,
        scratch_shapes=ROTATION_SCRATCH + [pltpu.VMEM((2, 3, TILE, TILE), BF16)],
        compiler_params=params(),
        cost_estimate=cost(2 * WIDE**3, 4 * 2**20),
        name="rotation_two",
    )(flags, recv_diag, keep_diag, top, low)


CHUNK = 512


def half_kernel(half_ref, cols_ref, rot_ref, out_ref):
    out_ref[...] = jnp.dot(cols_ref[...], rot_ref[...], preferred_element_type=F32).astype(BF16)


def apply_half(half, cols, rotation, name):
    return pl.pallas_call(
        half_kernel,
        out_shape=struct((ROWS, HALF), BF16),
        grid_spec=pltpu.PrefetchScalarGridSpec(
            num_scalar_prefetch=1,
            grid=(ROWS // CHUNK,),
            in_specs=[
                pl.BlockSpec((CHUNK, WIDE), lambda k, half: (k, 0)),
                pl.BlockSpec((WIDE, HALF), lambda k, half: (0, half[0])),
            ],
            out_specs=pl.BlockSpec((CHUNK, HALF), lambda k, half: (k, 0)),
        ),
        compiler_params=params(),
        cost_estimate=cost(ROWS * WIDE * HALF, ROWS * WIDE * 2 + ROWS * HALF * 2 + 2**20),
        name=name,
    )(half, cols, rotation)


def diag_kernel(send_ref, keep_ref, mine_ref, other_ref):
    for place, (i, j) in enumerate(DIAG_TILES):
        at_i, at_j = pl.ds(i * TILE, TILE), pl.ds(j * TILE, TILE)
        mine_ref[place] = gram_dot(send_ref[:, at_i], send_ref[:, at_j])
        other_ref[place] = gram_dot(keep_ref[:, at_i], keep_ref[:, at_j]).astype(BF16)


def diag_grams(send, keep):
    return pl.pallas_call(
        diag_kernel,
        out_shape=(struct((3, TILE, TILE), F32), struct((3, TILE, TILE), BF16)),
        in_specs=[VMEM, VMEM],
        out_specs=(VMEM, VMEM),
        compiler_params=params(),
        cost_estimate=cost(6 * ROWS * TILE * TILE, 2 * ROWS * HALF * 2 + 2**20),
        name="diag_grams",
    )(send, keep)


def cross_kernel(first_ref, recv_ref, keep_ref, after_ref, top_ref, low_ref):
    def fill(left, right):
        top_ref[...] = gram_dot(left[:, :TILE], right[...]).astype(BF16)
        low_ref[...] = gram_dot(left[:, TILE:], right[...]).astype(BF16)

    @pl.when(first_ref[0] == 0)
    def _():
        fill(recv_ref, keep_ref)

    @pl.when(first_ref[0] != 0)
    def _():
        fill(keep_ref, recv_ref)


def cross_gram(first, recv, keep, after):
    return pl.pallas_call(
        cross_kernel,
        out_shape=(struct((TILE, HALF), BF16), struct((TILE, HALF), BF16)),
        in_specs=[SMEM, VMEM, VMEM, HBM],
        out_specs=(VMEM, VMEM),
        compiler_params=params(),
        cost_estimate=cost(4 * ROWS * TILE * TILE, 2 * ROWS * HALF * 2 + 2**19),
        name="cross_gram",
    )(first, recv, keep, after)


def both_kernel(places_ref, recv_ref, keep_ref, rot_recv, rot_keep, out_ref):
    out = jnp.dot(recv_ref[...], rot_recv[...], preferred_element_type=F32)
    out = out + jnp.dot(keep_ref[...], rot_keep[...], preferred_element_type=F32)
    out = out.astype(BF16)
    swap = places_ref[2]
    out_ref[:, :HALF] = jnp.where(swap == 1, out[:, HALF:], out[:, :HALF])
    out_ref[:, HALF:] = jnp.where(swap == 1, out[:, :HALF], out[:, HALF:])


def apply_both(places, recv, keep, rotation):
    return pl.pallas_call(
        both_kernel,
        out_shape=struct((ROWS, WIDE), BF16),
        grid_spec=pltpu.PrefetchScalarGridSpec(
            num_scalar_prefetch=1,
            grid=(ROWS // CHUNK,),
            in_specs=[
                pl.BlockSpec((CHUNK, HALF), lambda k, at: (k, 0)),
                pl.BlockSpec((CHUNK, HALF), lambda k, at: (k, 0)),
                pl.BlockSpec((HALF, WIDE), lambda k, at: (at[0], 0)),
                pl.BlockSpec((HALF, WIDE), lambda k, at: (at[1], 0)),
            ],
            out_specs=pl.BlockSpec((CHUNK, WIDE), lambda k, at: (k, 0)),
        ),
        compiler_params=params(60),
        cost_estimate=cost(ROWS * WIDE * WIDE, 2 * ROWS * WIDE * 2 + 2**21),
        name="apply_both",
    )(places, recv, keep, rotation, rotation)


def add(left, right):
    return (left.astype(F32) + right.astype(F32)).astype(BF16)


def local(weight):
    place = lax.axis_index(NODE_AXES)
    core = lax.axis_index("core")
    node = jnp.asarray(np.array(NODE_AT, np.int32))[place]
    core1 = core.astype(jnp.int32)[None]

    parts = lax.all_to_all(spread(weight), NODE_AXES, 0, 0, tiled=True)
    cols = parts.reshape(ROWS, WIDE)

    mine, other = gram(core1, cols)
    chip = add(mine, permute(other, CORE_SWAP))
    own = add(chip, permute(chip, Z_SWAP))
    rotation = rotation_one(core1, own, permute(own, CORE_SWAP))

    next_is_upper = node <= 16
    send_half = jnp.where(next_is_upper == (core == 0), 0, 1).astype(jnp.int32)
    send = apply_half(send_half[None], cols, rotation, "apply_send")
    recv = permute(send, RING_SEND)
    keep = apply_half(1 - send_half[None], cols, rotation, "apply_keep")

    mine, other = diag_grams(send, keep)
    chip = add(mine, permute(other, CORE_SWAP))
    send_diag = add(chip, permute(chip, Z_SWAP))
    keep_diag = permute(send_diag, CORE_SWAP)
    recv_diag = permute(send_diag, RING_SEND)

    edge = jnp.where(core == 0, (node + NODES - 1) % NODES, node)
    first_is_upper = (edge <= 15).astype(jnp.int32)
    top, low = cross_gram(core1, recv, keep, keep_diag)
    top, low = add(top, permute(top, CHAIN_SWAP)), add(low, permute(low, Z_SWAP))
    top, low = add(top, permute(top, Z_SWAP)), add(low, permute(low, CHAIN_SWAP))
    flags = jnp.stack([core1[0], first_is_upper])
    rotation = rotation_two(flags, recv_diag, keep_diag, top, low)
    places = jnp.stack([core1[0], 1 - core1[0], 1 - first_is_upper])
    cols = apply_both(places, recv, keep, rotation)

    parts = lax.all_to_all(cols.reshape(NODES, PER, WIDE), NODE_AXES, 0, 0, tiled=True)
    pairs = [[edge_pair((NODE_AT[n] - 1 + c) % NODES) for n in range(NODES)] for c in range(2)]
    source = np.array([[row.index(q) for q in range(NODES)] for row in pairs], np.int32)
    return gather(parts, jnp.asarray(source)[core])


def solution(mesh):
    fine = Mesh(mesh.devices.reshape(4, 2, 4, 2, 2), AXES)
    return jax.shard_map(
        local,
        mesh=fine,
        in_specs=(P(AXES, None),),
        out_specs=P(AXES, None),
        check_vma=False,
    )
```

```python
import jax
import jax.numpy as jnp
import numpy as np
from jax import lax
from jax.experimental import pallas as pl
from jax.experimental.pallas import tpu as pltpu
from jax.sharding import Mesh
from jax.sharding import PartitionSpec as P

NODES = 16
HALF = 512
WIDE = 1024
TILE = 256
PER = 64
ROWS = NODES * PER
AXES = ("x", "zh", "y", "zl", "core")
NODE_AXES = ("x", "y")
F32 = jnp.float32
BF16 = jnp.bfloat16
VMEM = pl.BlockSpec(memory_space=pltpu.VMEM)
SMEM = pl.BlockSpec(memory_space=pltpu.SMEM)
HBM = pl.BlockSpec(memory_space=pl.ANY)

RING = [0] + list(range(1, 32, 2)) + list(range(30, 0, -2))


def node_places():
    places = []
    for x in range(4):
        places += [x * 4 + (y if x % 2 == 0 else 3 - y) for y in range(4)]
    return places


PLACE = node_places()
NODE_AT = [PLACE.index(n) for n in range(NODES)]


def edge_pair(edge):
    return 2 * edge if edge <= 15 else 63 - 2 * edge


def flat(place, z, core):
    x, y = divmod(place, 4)
    zh, zl = divmod(z, 2)
    return (((x * 2 + zh) * 4 + y) * 2 + zl) * 2 + core


def all_perm(target):
    return [
        (flat(PLACE[j], z, c), flat(*target(j, z, c)))
        for j in range(NODES)
        for z in range(4)
        for c in range(2)
    ]


CORE_SWAP = all_perm(lambda j, z, c: (PLACE[j], z, 1 - c))
Z_EVEN = all_perm(lambda j, z, c: (PLACE[j], z ^ 1, c))
Z_ODD = all_perm(lambda j, z, c: (PLACE[j], 3 - z, c))
RING_BACK = all_perm(lambda j, z, c: (PLACE[(j - 1) % NODES], z, c))


def permute(value, table):
    return lax.ppermute(value, AXES, table)


def params(mebibytes=40):
    return pltpu.CompilerParams(vmem_limit_bytes=mebibytes * 1024 * 1024)


def cost(macs, nbytes):
    return pl.CostEstimate(flops=2 * macs, bytes_accessed=nbytes, transcendentals=0)


def struct(shape, dtype):
    return jax.ShapeDtypeStruct(shape, dtype)


def gram_dot(left, right):
    return lax.dot_general(left, right, (((0,), (0,)), ((), ())), preferred_element_type=F32)


GROUP = 4
STAGE = [pltpu.VMEM((NODES, PER, WIDE), BF16)]
STAGE += [pltpu.SemaphoreType.DMA((NODES,)), pltpu.SemaphoreType.DMA((NODES,))]


def spread(weight, first, name):
    def kernel(weight_ref, out_ref, held, load_sems, store_sems):
        loads, stores = [], []
        for n in range(NODES):
            pair = RING[2 * NODE_AT[n] + first]
            columns = weight_ref.at[:, pl.ds(pair * WIDE, WIDE)]
            loads.append(pltpu.make_async_copy(columns, held.at[n], load_sems.at[n]))
        for k in range(NODES // GROUP):
            at = pl.ds(k * GROUP, GROUP)
            stores.append(pltpu.make_async_copy(held.at[at], out_ref.at[at], store_sems.at[k]))
        for load in loads:
            load.start()
        for k, store in enumerate(stores):
            for load in loads[GROUP * k : GROUP * (k + 1)]:
                load.wait()
            store.start()
        for store in stores:
            store.wait()

    return pl.pallas_call(
        kernel,
        out_shape=struct((NODES, PER, WIDE), BF16),
        in_specs=[HBM],
        out_specs=HBM,
        scratch_shapes=STAGE,
        compiler_params=params(60),
        cost_estimate=cost(0, 2 * ROWS * WIDE * 2),
        name=name,
    )(weight)


def gather(parts, first, whole, name):
    def kernel(parts_ref, *refs):
        out_ref, held, load_sems, store_sems = refs[-4:]
        loads, stores = [], []
        for n in range(NODES):
            pair = edge_pair(2 * NODE_AT[n] + first)
            columns = out_ref.at[:, pl.ds(pair * WIDE, WIDE)]
            loads.append(pltpu.make_async_copy(parts_ref.at[n], held.at[n], load_sems.at[n]))
            stores.append(pltpu.make_async_copy(held.at[n], columns, store_sems.at[n]))
        for load in loads:
            load.start()
        for load, store in zip(loads, stores):
            load.wait()
            store.start()
        for store in stores:
            store.wait()

    operands = (parts,) if whole is None else (parts, whole)
    return pl.pallas_call(
        kernel,
        out_shape=struct((PER, 2 * NODES * WIDE), BF16),
        in_specs=[HBM] * len(operands),
        out_specs=HBM,
        scratch_shapes=STAGE,
        input_output_aliases={} if whole is None else {1: 0},
        compiler_params=params(60),
        cost_estimate=cost(0, 2 * ROWS * WIDE * 2),
        name=name,
    )(*operands)


TILES = [(0, 0), (0, 1), (1, 1), (0, 2), (0, 3), (2, 2), (2, 3), (3, 3), (1, 2), (1, 3)]


def gram_body(core, first, second, mine_ref, other_ref):
    def put(row, col, tile):
        owner, slot = divmod(TILES.index((row, col)), 5)
        for half in range(2):
            part = tile[half * 128 : (half + 1) * 128]

            @pl.when(core == owner)
            def _():
                mine_ref[2 * slot + half] = part

            @pl.when(core != owner)
            def _():
                other_ref[2 * slot + half] = part.astype(BF16)

    for block, cols in ((0, first), (2, second)):
        for i in range(2):
            left = cols[:, i * TILE : (i + 1) * TILE]
            strip = gram_dot(left, cols[:, i * TILE :])
            for j in range(i, 2):
                put(block + i, block + j, strip[:, (j - i) * TILE : (j - i + 1) * TILE])
            if block == 0:
                strip = gram_dot(left, second[...])
                for j in range(2):
                    put(i, 2 + j, strip[:, j * TILE : (j + 1) * TILE])


def gram_whole_kernel(core_ref, cols_ref, after_ref, mine_ref, other_ref):
    first, second = cols_ref.at[:, pl.ds(0, HALF)], cols_ref.at[:, pl.ds(HALF, HALF)]
    gram_body(core_ref[0], first, second, mine_ref, other_ref)


def gram_halves_kernel(core_ref, first_ref, second_ref, after_ref, mine_ref, other_ref):
    gram_body(core_ref[0], first_ref, second_ref, mine_ref, other_ref)


def gram(core, cols, after, name):
    return pl.pallas_call(
        gram_whole_kernel if len(cols) == 1 else gram_halves_kernel,
        out_shape=(struct((10, 128, TILE), F32), struct((10, 128, TILE), BF16)),
        in_specs=[SMEM] + [VMEM] * len(cols) + [HBM],
        out_specs=(VMEM, VMEM),
        compiler_params=params(),
        cost_estimate=cost(10 * ROWS * TILE * TILE, ROWS * WIDE * 2 + 2**21),
        name=name,
    )(core, *cols, after)


def mixed_kernel(core_ref, done_ref, cols_ref, mine_ref, other_ref):
    for i in range(2):
        strip = gram_dot(done_ref[:, i * TILE : (i + 1) * TILE], cols_ref[...])
        for half in range(2):
            part = strip[half * 128 : (half + 1) * 128]

            @pl.when(core_ref[0] == i)
            def _():
                mine_ref[half] = part

            @pl.when(core_ref[0] != i)
            def _():
                other_ref[half] = part.astype(BF16)


def mixed(core, done, cols, name):
    return pl.pallas_call(
        mixed_kernel,
        out_shape=(struct((2, 128, WIDE), F32), struct((2, 128, WIDE), BF16)),
        in_specs=[SMEM, VMEM, VMEM],
        out_specs=(VMEM, VMEM),
        compiler_params=params(),
        cost_estimate=cost(ROWS * HALF * WIDE, ROWS * WIDE * 3 + 2**21),
        name=name,
    )(core, done, cols)


def add(left, right):
    return (left.astype(F32) + right.astype(F32)).astype(BF16)


def total(mine, other):
    far = permute(other, CORE_SWAP)
    cut = other.shape[0] // 2
    low, high = add(mine[:cut], far[:cut]), add(mine[cut:], far[cut:])
    low, high = add(low, permute(low, Z_EVEN)), add(high, permute(high, Z_ODD))
    low, high = add(low, permute(low, Z_ODD)), add(high, permute(high, Z_EVEN))
    return low, high, permute(low, CORE_SWAP), permute(high, CORE_SWAP)


def rotation_body(tiles, sign, slot, rot_ref, gen, gen_low, middle):
    rows = lax.broadcasted_iota(jnp.int32, (TILE, TILE), 0)
    cols = lax.broadcasted_iota(jnp.int32, (TILE, TILE), 1)
    down, across = [], []
    for i in range(4):
        only = jnp.where(rows == cols, tiles(i, i), 0.0)
        down.append(jnp.sum(only, axis=1, keepdims=True))
        across.append(jnp.sum(only, axis=0, keepdims=True))
    total = jnp.zeros((TILE, TILE), F32)
    for i in range(4):
        for j in range(i, 4):
            upper = tiles(i, j) / (down[i] + across[j] + 0.001)
            if i == j:
                upper = jnp.where(rows < cols, upper, 0.0)
            elif i < 2 <= j:
                upper = upper * sign
            total = total + upper * upper
            at_i, at_j = pl.ds(i * TILE, TILE), pl.ds(j * TILE, TILE)
            if i == j:
                both = upper - upper.T
                gen[at_i, at_j] = both
                gen_low[at_i, at_j] = both.astype(BF16)
            else:
                flipped = -upper.T
                gen[at_i, at_j] = upper
                gen_low[at_i, at_j] = upper.astype(BF16)
                gen[at_j, at_i] = flipped
                gen_low[at_j, at_i] = flipped.astype(BF16)
    norm_sq = 1.0 + 2.0 * jnp.sum(total, keepdims=True) / WIDE
    inv_norm = lax.rsqrt(norm_sq)
    scale = 0.5 * inv_norm * inv_norm
    wide_rows = lax.broadcasted_iota(jnp.int32, (TILE, WIDE), 0)
    wide_cols = lax.broadcasted_iota(jnp.int32, (TILE, WIDE), 1)
    for i in range(4):
        at = pl.ds(i * TILE, TILE)
        squared = jnp.dot(gen_low[at, :], gen_low[...], preferred_element_type=F32)
        identity = jnp.where(wide_rows + i * TILE == wide_cols, 1.0, 0.0)
        middle[at, :] = (1.5 * identity - scale * (identity - squared)).astype(BF16)
    for i in range(4):
        at = pl.ds(i * TILE, TILE)
        identity = jnp.where(wide_rows + i * TILE == wide_cols, 1.0, 0.0)
        start_rot = ((identity + gen[at, :]) * inv_norm).astype(BF16)
        strip = jnp.dot(start_rot, middle[...], preferred_element_type=F32).astype(BF16)
        rot_ref[slot, at, :] = strip[:, :HALF]
        rot_ref[1 - slot, at, :] = strip[:, HALF:]


ROTATION_SCRATCH = [
    pltpu.VMEM((WIDE, WIDE), F32),
    pltpu.VMEM((WIDE, WIDE), BF16),
    pltpu.VMEM((WIDE, WIDE), BF16),
]


def hold(core, sums, held):
    own_low, own_high, far_low, far_high = sums
    cut = own_low.shape[0]
    held[core, :cut] = own_low[...]
    held[core, cut:] = own_high[...]
    held[1 - core, :cut] = far_low[...]
    held[1 - core, cut:] = far_high[...]


def held_tile(held, i, j):
    owner, slot = divmod(TILES.index((i, j)), 5)
    return held[owner, 2 * slot : 2 * slot + 2].reshape(TILE, TILE)


HELD = [pltpu.VMEM((2, 10, 128, TILE), BF16)]
DIAG = [(0, 0), (0, 1), (1, 1)]


def rotation_kernel(flags_ref, *refs):
    rot_ref, gen, gen_low, middle, held = refs[4:]
    hold(flags_ref[0], refs[:4], held)
    sign = jnp.where(flags_ref[1] == 1, 1.0, -1.0)

    def tiles(i, j):
        return held_tile(held, i, j).astype(F32)

    rotation_body(tiles, sign, 1 - flags_ref[1], rot_ref, gen, gen_low, middle)


def rotation(flags, sums, name):
    return pl.pallas_call(
        rotation_kernel,
        out_shape=struct((2, WIDE, HALF), BF16),
        in_specs=[SMEM] + [VMEM] * 4,
        out_specs=VMEM,
        scratch_shapes=ROTATION_SCRATCH + HELD,
        compiler_params=params(),
        cost_estimate=cost(2 * WIDE**3, 4 * 2**20),
        name=name,
    )(flags, *sums)


def rotation_diag_kernel(flags_ref, *refs):
    rot_ref, diag_ref, gen, gen_low, middle, held, gram_all, turned = refs[4:]
    hold(flags_ref[0], refs[:4], held)

    def tiles(i, j):
        return held_tile(held, i, j).astype(F32)

    rotation_body(tiles, 1.0, 0, rot_ref, gen, gen_low, middle)
    for i in range(4):
        for j in range(i, 4):
            at_i, at_j = pl.ds(i * TILE, TILE), pl.ds(j * TILE, TILE)
            tile = held_tile(held, i, j)
            gram_all[at_i, at_j] = tile
            if i != j:
                gram_all[at_j, at_i] = tile.astype(F32).T.astype(BF16)
    rot = rot_ref.at[flags_ref[2]]
    for i in range(4):
        at = pl.ds(i * TILE, TILE)
        turned[at, :] = jnp.dot(gram_all[at, :], rot[...], preferred_element_type=F32).astype(BF16)
    for place, (i, j) in enumerate(DIAG):
        at_i, at_j = pl.ds(i * TILE, TILE), pl.ds(j * TILE, TILE)
        diag_ref[place] = gram_dot(rot[:, at_i], turned[:, at_j])


def rotation_diag(flags, sums, name):
    return pl.pallas_call(
        rotation_diag_kernel,
        out_shape=(struct((2, WIDE, HALF), BF16), struct((3, TILE, TILE), F32)),
        in_specs=[SMEM] + [VMEM] * 4,
        out_specs=(VMEM, VMEM),
        scratch_shapes=ROTATION_SCRATCH
        + HELD
        + [pltpu.VMEM((WIDE, WIDE), BF16), pltpu.VMEM((WIDE, HALF), BF16)],
        compiler_params=params(),
        cost_estimate=cost(3 * WIDE**3, 6 * 2**20),
        name=name,
    )(flags, *sums)


def rotation_mixed_kernel(flags_ref, rot_b, diag_a, diag_b, *refs):
    rot_ref, gen, gen_low, middle, held, cross = refs[4:]
    hold(flags_ref[0], refs[:4], held)
    sign = jnp.where(flags_ref[1] == 1, 1.0, -1.0)
    for i in range(2):
        strip = held[i].reshape(TILE, WIDE)
        cross[i] = jnp.dot(strip, rot_b[flags_ref[2]], preferred_element_type=F32)

    def tiles(i, j):
        if i < 2 <= j:
            return cross[i, :, (j - 2) * TILE : (j - 1) * TILE]
        if j < 2:
            return diag_a[DIAG.index((i, j))]
        return diag_b[DIAG.index((i - 2, j - 2))]

    rotation_body(tiles, sign, 1 - flags_ref[1], rot_ref, gen, gen_low, middle)


def rotation_mixed(flags, rot_b, diag_a, diag_b, sums, name):
    return pl.pallas_call(
        rotation_mixed_kernel,
        out_shape=struct((2, WIDE, HALF), BF16),
        in_specs=[SMEM] + [VMEM] * 7,
        out_specs=VMEM,
        scratch_shapes=ROTATION_SCRATCH
        + [pltpu.VMEM((2, 2, 128, WIDE), BF16), pltpu.VMEM((2, TILE, HALF), F32)],
        compiler_params=params(),
        cost_estimate=cost(2 * WIDE**3 + WIDE**3 // 4, 6 * 2**20),
        name=name,
    )(flags, rot_b, diag_a, diag_b, *sums)


CHUNK = 256


def half_kernel(half_ref, cols_ref, rot_ref, out_ref):
    half = half_ref[0]
    for k in range(ROWS // CHUNK):
        at = pl.ds(k * CHUNK, CHUNK)
        out = jnp.dot(cols_ref[at, :], rot_ref[half], preferred_element_type=F32)
        out_ref[at, :] = out.astype(BF16)


def apply_half(half, cols, rot, name):
    return pl.pallas_call(
        half_kernel,
        out_shape=struct((ROWS, HALF), BF16),
        in_specs=[SMEM, VMEM, VMEM],
        out_specs=VMEM,
        compiler_params=params(),
        cost_estimate=cost(ROWS * WIDE * HALF, ROWS * WIDE * 3 + 2**20),
        name=name,
    )(half, cols, rot)


def both_kernel(first_ref, second_ref, rot_ref, out_ref):
    for k in range(ROWS // CHUNK):
        at = pl.ds(k * CHUNK, CHUNK)
        for half in range(2):
            out = jnp.dot(first_ref[at, :], rot_ref[half, :HALF], preferred_element_type=F32)
            out += jnp.dot(second_ref[at, :], rot_ref[half, HALF:], preferred_element_type=F32)
            out_ref[at, half * HALF : (half + 1) * HALF] = out.astype(BF16)


def apply_both(first, second, rot, name):
    return pl.pallas_call(
        both_kernel,
        out_shape=struct((ROWS, WIDE), BF16),
        in_specs=[VMEM] * 3,
        out_specs=VMEM,
        compiler_params=params(),
        cost_estimate=cost(ROWS * WIDE * WIDE, 2 * ROWS * WIDE * 2 + 2**21),
        name=name,
    )(first, second, rot)


def exchange(parts):
    return lax.all_to_all(parts, NODE_AXES, 0, 0, tiled=True)


def local(weight):
    core = lax.axis_index("core").astype(jnp.int32)
    node = jnp.asarray(np.array(NODE_AT, np.int32))[lax.axis_index(NODE_AXES)]
    core1 = core[None]

    def flags(first_is_upper, half=0):
        return jnp.stack([core, jnp.asarray(first_is_upper, jnp.int32), jnp.asarray(half, jnp.int32)])

    half_a = jnp.where(2 * node <= 16, 0, 1).astype(jnp.int32)
    half_b = jnp.where(2 * node + 1 <= 16, 1, 0).astype(jnp.int32)

    cols_a = exchange(spread(weight, 0, "spread_a")).reshape(ROWS, WIDE)
    cols_b = exchange(spread(weight, 1, "spread_b")).reshape(ROWS, WIDE)
    sums = total(*gram(core1, (cols_a,), cols_a, "gram_a"))
    rot_a, diag_a = rotation_diag(flags(1, half_a), sums, "rotation_a")
    prev_a = apply_half(1 - half_a[None], cols_a, rot_a, "apply_a_prev")
    far_a = permute(prev_a, RING_BACK)
    in_a = apply_half(half_a[None], cols_a, rot_a, "apply_a_in")

    sums_b = total(*gram(core1, (cols_b,), sums[1], "gram_b"))
    sums_mixed = total(*mixed(core1, in_a, cols_b, "mixed"))
    rot_b, diag_b = rotation_diag(flags(1, half_b), sums_b, "rotation_b")
    in_b = apply_half(half_b[None], cols_b, rot_b, "apply_b_in")
    next_b = apply_half(1 - half_b[None], cols_b, rot_b, "apply_b_next")

    rot = rotation_mixed(
        flags(2 * node <= 15, half_b), rot_b, diag_a, diag_b, sums_mixed, "rotation_in"
    )
    parts = apply_both(in_a, in_b, rot, "apply_in").reshape(NODES, PER, WIDE)
    parts_in = exchange(parts)

    sums = total(*gram(core1, (next_b, far_a), sums_mixed[3], "gram_off"))
    rot = rotation(flags(2 * node + 1 <= 15), sums, "rotation_off")
    parts = apply_both(next_b, far_a, rot, "apply_off").reshape(NODES, PER, WIDE)
    parts_off = exchange(parts)

    return gather(parts_off, 1, gather(parts_in, 0, None, "gather_in"), "gather_off")


def solution(mesh):
    fine = Mesh(mesh.devices.reshape(4, 2, 4, 2, 2), AXES)
    return jax.shard_map(
        local,
        mesh=fine,
        in_specs=(P(AXES, None),),
        out_specs=P(AXES, None),
        check_vma=False,
    )
```

```python
import jax
import jax.numpy as jnp
import numpy as np
from jax import lax
from jax.experimental import pallas as pl
from jax.experimental.pallas import tpu as pltpu
from jax.sharding import Mesh
from jax.sharding import PartitionSpec as P

NODES = 16
HALF = 512
WIDE = 1024
TILE = 256
PER = 64
ROWS = NODES * PER
AXES = ("x", "zh", "y", "zl", "core")
NODE_AXES = ("x", "y")
F32 = jnp.float32
BF16 = jnp.bfloat16
VMEM = pl.BlockSpec(memory_space=pltpu.VMEM)
SMEM = pl.BlockSpec(memory_space=pltpu.SMEM)
HBM = pl.BlockSpec(memory_space=pl.ANY)

RING = [0] + list(range(1, 32, 2)) + list(range(30, 0, -2))


def node_places():
    places = []
    for x in range(4):
        places += [x * 4 + (y if x % 2 == 0 else 3 - y) for y in range(4)]
    return places


PLACE = node_places()
NODE_AT = [PLACE.index(n) for n in range(NODES)]


def edge_pair(edge):
    return 2 * edge if edge <= 15 else 63 - 2 * edge


def flat(place, z, core):
    x, y = divmod(place, 4)
    zh, zl = divmod(z, 2)
    return (((x * 2 + zh) * 4 + y) * 2 + zl) * 2 + core


def all_perm(target):
    return [
        (flat(PLACE[j], z, c), flat(*target(j, z, c)))
        for j in range(NODES)
        for z in range(4)
        for c in range(2)
    ]


CORE_SWAP = all_perm(lambda j, z, c: (PLACE[j], z, 1 - c))
Z_EVEN = all_perm(lambda j, z, c: (PLACE[j], z ^ 1, c))
Z_ODD = all_perm(lambda j, z, c: (PLACE[j], 3 - z, c))
RING_BACK = all_perm(lambda j, z, c: (PLACE[(j - 1) % NODES], z, c))


def permute(value, table):
    return lax.ppermute(value, AXES, table)


def params(mebibytes=40):
    return pltpu.CompilerParams(vmem_limit_bytes=mebibytes * 1024 * 1024)


def cost(macs, nbytes):
    return pl.CostEstimate(flops=2 * macs, bytes_accessed=nbytes, transcendentals=0)


def struct(shape, dtype):
    return jax.ShapeDtypeStruct(shape, dtype)


def gram_dot(left, right):
    return lax.dot_general(left, right, (((0,), (0,)), ((), ())), preferred_element_type=F32)


GROUP = 4


def spread_kernel(weight_ref, *refs):
    outs, (held, load_sems, store_sems) = refs[:2], refs[2:]
    loads, stores = [], []
    for first, out_ref in enumerate(outs):
        for n in range(NODES):
            pair, place = RING[2 * NODE_AT[n] + first], first * NODES + n
            columns = weight_ref.at[:, pl.ds(pair * WIDE, WIDE)]
            loads.append(pltpu.make_async_copy(columns, held.at[place], load_sems.at[place]))
        for k in range(0, NODES, GROUP):
            place = first * NODES + k
            source, target = held.at[pl.ds(place, GROUP)], out_ref.at[pl.ds(k, GROUP)]
            stores.append(pltpu.make_async_copy(source, target, store_sems.at[place]))
    for load in loads:
        load.start()
    for k, store in enumerate(stores):
        for load in loads[GROUP * k : GROUP * (k + 1)]:
            load.wait()
        store.start()
    for store in stores:
        store.wait()


def spread(weight):
    out = struct((NODES, PER, WIDE), BF16)
    return pl.pallas_call(
        spread_kernel,
        out_shape=(out, out),
        in_specs=[HBM],
        out_specs=(HBM, HBM),
        scratch_shapes=[
            pltpu.VMEM((2 * NODES, PER, WIDE), BF16),
            pltpu.SemaphoreType.DMA((2 * NODES,)),
            pltpu.SemaphoreType.DMA((2 * NODES,)),
        ],
        compiler_params=params(60),
        cost_estimate=cost(0, 4 * ROWS * WIDE * 2),
        name="spread",
    )(weight)


def gather(parts, first, whole, name):
    def kernel(parts_ref, *refs):
        out_ref, sems = refs[-2:]
        stores = []
        for n in range(NODES):
            pair = edge_pair(2 * NODE_AT[n] + first)
            columns = out_ref.at[:, pl.ds(pair * WIDE, WIDE)]
            stores.append(pltpu.make_async_copy(parts_ref.at[n], columns, sems.at[n]))
        for store in stores:
            store.start()
        for store in stores:
            store.wait()

    operands = (parts,) if whole is None else (parts, whole)
    return pl.pallas_call(
        kernel,
        out_shape=struct((PER, 2 * NODES * WIDE), BF16),
        in_specs=[VMEM, HBM][: len(operands)],
        out_specs=HBM,
        scratch_shapes=[pltpu.SemaphoreType.DMA((NODES,))],
        input_output_aliases={} if whole is None else {1: 0},
        compiler_params=params(),
        cost_estimate=cost(0, 2 * ROWS * WIDE * 2),
        name=name,
    )(*operands)


TILES = [(0, 0), (0, 1), (1, 1), (0, 2), (0, 3), (2, 2), (2, 3), (3, 3), (1, 2), (1, 3)]


def gram_body(core, first, second, mine_ref, other_ref):
    def put(row, col, tile):
        owner, slot = divmod(TILES.index((row, col)), 5)
        for half in range(2):
            part = tile[half * 128 : (half + 1) * 128]

            @pl.when(core == owner)
            def _():
                mine_ref[2 * slot + half] = part

            @pl.when(core != owner)
            def _():
                other_ref[2 * slot + half] = part.astype(BF16)

    for block, cols in ((0, first), (2, second)):
        for i in range(2):
            left = cols[:, i * TILE : (i + 1) * TILE]
            strip = gram_dot(left, cols[:, i * TILE :])
            for j in range(i, 2):
                put(block + i, block + j, strip[:, (j - i) * TILE : (j - i + 1) * TILE])
            if block == 0:
                strip = gram_dot(left, second[...])
                for j in range(2):
                    put(i, 2 + j, strip[:, j * TILE : (j + 1) * TILE])


def gram_whole_kernel(core_ref, cols_ref, after_ref, mine_ref, other_ref):
    first, second = cols_ref.at[:, pl.ds(0, HALF)], cols_ref.at[:, pl.ds(HALF, HALF)]
    gram_body(core_ref[0], first, second, mine_ref, other_ref)


def gram_halves_kernel(core_ref, first_ref, second_ref, after_ref, mine_ref, other_ref):
    gram_body(core_ref[0], first_ref, second_ref, mine_ref, other_ref)


def gram(core, cols, after, name):
    return pl.pallas_call(
        gram_whole_kernel if len(cols) == 1 else gram_halves_kernel,
        out_shape=(struct((10, 128, TILE), F32), struct((10, 128, TILE), BF16)),
        in_specs=[SMEM] + [VMEM] * len(cols) + [HBM],
        out_specs=(VMEM, VMEM),
        compiler_params=params(),
        cost_estimate=cost(ROWS * TILE, ROWS * WIDE // 8),
        name=name,
    )(core, *cols, after)


def mixed_kernel(core_ref, done_ref, cols_ref, mine_ref, other_ref):
    for i in range(2):
        strip = gram_dot(done_ref[:, i * TILE : (i + 1) * TILE], cols_ref[...])
        for half in range(2):
            part = strip[half * 128 : (half + 1) * 128]

            @pl.when(core_ref[0] == i)
            def _():
                mine_ref[half] = part

            @pl.when(core_ref[0] != i)
            def _():
                other_ref[half] = part.astype(BF16)


def mixed(core, done, cols, name):
    return pl.pallas_call(
        mixed_kernel,
        out_shape=(struct((2, 128, WIDE), F32), struct((2, 128, WIDE), BF16)),
        in_specs=[SMEM, VMEM, VMEM],
        out_specs=(VMEM, VMEM),
        compiler_params=params(),
        cost_estimate=cost(ROWS * HALF * WIDE, ROWS * WIDE * 3 + 2**21),
        name=name,
    )(core, done, cols)


def add(left, right):
    return (left.astype(F32) + right.astype(F32)).astype(BF16)


def total(mine, other):
    far = permute(other, CORE_SWAP)
    cut = other.shape[0] // 2
    low, high = add(mine[:cut], far[:cut]), add(mine[cut:], far[cut:])
    midway, high = add(low, permute(low, Z_EVEN)), add(high, permute(high, Z_ODD))
    low, high = add(midway, permute(midway, Z_ODD)), add(high, permute(high, Z_EVEN))
    return (low, high, permute(low, CORE_SWAP), permute(high, CORE_SWAP)), midway


def rotation_body(tiles, sign, slot, rot_ref, gen, gen_low, middle):
    rows = lax.broadcasted_iota(jnp.int32, (TILE, TILE), 0)
    cols = lax.broadcasted_iota(jnp.int32, (TILE, TILE), 1)
    down, across = [], []
    for i in range(4):
        only = jnp.where(rows == cols, tiles(i, i), 0.0)
        down.append(jnp.sum(only, axis=1, keepdims=True))
        across.append(jnp.sum(only, axis=0, keepdims=True))
    total = jnp.zeros((TILE, TILE), F32)
    for i in range(4):
        for j in range(i, 4):
            upper = tiles(i, j) / (down[i] + across[j] + 0.001)
            if i == j:
                upper = jnp.where(rows < cols, upper, 0.0)
            elif i < 2 <= j:
                upper = upper * sign
            total = total + upper * upper
            at_i, at_j = pl.ds(i * TILE, TILE), pl.ds(j * TILE, TILE)
            if i == j:
                both = upper - upper.T
                gen[at_i, at_j] = both
                gen_low[at_i, at_j] = both.astype(BF16)
            else:
                flipped = -upper.T
                gen[at_i, at_j] = upper
                gen_low[at_i, at_j] = upper.astype(BF16)
                gen[at_j, at_i] = flipped
                gen_low[at_j, at_i] = flipped.astype(BF16)
    norm_sq = 1.0 + 2.0 * jnp.sum(total, keepdims=True) / WIDE
    inv_norm = lax.rsqrt(norm_sq)
    scale = 0.5 * inv_norm * inv_norm
    wide_rows = lax.broadcasted_iota(jnp.int32, (TILE, WIDE), 0)
    wide_cols = lax.broadcasted_iota(jnp.int32, (TILE, WIDE), 1)
    for i in range(4):
        at = pl.ds(i * TILE, TILE)
        squared = jnp.dot(gen_low[at, :], gen_low[...], preferred_element_type=F32)
        identity = jnp.where(wide_rows + i * TILE == wide_cols, 1.0, 0.0)
        middle[at, :] = (1.5 * identity - scale * (identity - squared)).astype(BF16)
    for i in range(4):
        at = pl.ds(i * TILE, TILE)
        identity = jnp.where(wide_rows + i * TILE == wide_cols, 1.0, 0.0)
        start_rot = ((identity + gen[at, :]) * inv_norm).astype(BF16)
        strip = jnp.dot(start_rot, middle[...], preferred_element_type=F32).astype(BF16)
        rot_ref[slot, at, :] = strip[:, :HALF]
        rot_ref[1 - slot, at, :] = strip[:, HALF:]


ROTATION_SCRATCH = [
    pltpu.VMEM((WIDE, WIDE), F32),
    pltpu.VMEM((WIDE, WIDE), BF16),
    pltpu.VMEM((WIDE, WIDE), BF16),
]


def hold(core, sums, held):
    own_low, own_high, far_low, far_high = sums
    cut = own_low.shape[0]
    held[core, :cut] = own_low[...]
    held[core, cut:] = own_high[...]
    held[1 - core, :cut] = far_low[...]
    held[1 - core, cut:] = far_high[...]


def held_tile(held, i, j):
    owner, slot = divmod(TILES.index((i, j)), 5)
    return held[owner, 2 * slot : 2 * slot + 2].reshape(TILE, TILE)


HELD = [pltpu.VMEM((2, 10, 128, TILE), BF16)]
DIAG = [(0, 0), (0, 1), (1, 1)]


def rotation_kernel(flags_ref, *refs):
    rot_ref, gen, gen_low, middle, held = refs[4:]
    hold(flags_ref[0], refs[:4], held)
    sign = jnp.where(flags_ref[1] == 1, 1.0, -1.0)

    def tiles(i, j):
        return held_tile(held, i, j).astype(F32)

    rotation_body(tiles, sign, 1 - flags_ref[1], rot_ref, gen, gen_low, middle)


def rotation(flags, sums, name):
    return pl.pallas_call(
        rotation_kernel,
        out_shape=struct((2, WIDE, HALF), BF16),
        in_specs=[SMEM] + [VMEM] * 4,
        out_specs=VMEM,
        scratch_shapes=ROTATION_SCRATCH + HELD,
        compiler_params=params(),
        cost_estimate=cost(2 * WIDE**3, 4 * 2**20),
        name=name,
    )(flags, *sums)


def rotation_diag_kernel(flags_ref, *refs):
    rot_ref, diag_ref, gen, gen_low, middle, held, gram_all, turned = refs[4:]
    hold(flags_ref[0], refs[:4], held)

    def tiles(i, j):
        return held_tile(held, i, j).astype(F32)

    rotation_body(tiles, 1.0, 0, rot_ref, gen, gen_low, middle)
    for i in range(4):
        for j in range(i, 4):
            at_i, at_j = pl.ds(i * TILE, TILE), pl.ds(j * TILE, TILE)
            tile = held_tile(held, i, j)
            gram_all[at_i, at_j] = tile
            if i != j:
                gram_all[at_j, at_i] = tile.astype(F32).T.astype(BF16)
    rot = rot_ref.at[flags_ref[2]]
    for i in range(4):
        at = pl.ds(i * TILE, TILE)
        turned[at, :] = jnp.dot(gram_all[at, :], rot[...], preferred_element_type=F32).astype(BF16)
    for place, (i, j) in enumerate(DIAG):
        at_i, at_j = pl.ds(i * TILE, TILE), pl.ds(j * TILE, TILE)
        diag_ref[place] = gram_dot(rot[:, at_i], turned[:, at_j])


def rotation_diag(flags, sums, name):
    return pl.pallas_call(
        rotation_diag_kernel,
        out_shape=(struct((2, WIDE, HALF), BF16), struct((3, TILE, TILE), F32)),
        in_specs=[SMEM] + [VMEM] * 4,
        out_specs=(VMEM, VMEM),
        scratch_shapes=ROTATION_SCRATCH
        + HELD
        + [pltpu.VMEM((WIDE, WIDE), BF16), pltpu.VMEM((WIDE, HALF), BF16)],
        compiler_params=params(),
        cost_estimate=cost(3 * WIDE**3, 6 * 2**20),
        name=name,
    )(flags, *sums)


def rotation_mixed_kernel(flags_ref, rot_b, diag_a, diag_b, *refs):
    rot_ref, gen, gen_low, middle, held, cross = refs[4:]
    hold(flags_ref[0], refs[:4], held)
    sign = jnp.where(flags_ref[1] == 1, 1.0, -1.0)
    for i in range(2):
        strip = held[i].reshape(TILE, WIDE)
        cross[i] = jnp.dot(strip, rot_b[flags_ref[2]], preferred_element_type=F32)

    def tiles(i, j):
        if i < 2 <= j:
            return cross[i, :, (j - 2) * TILE : (j - 1) * TILE]
        if j < 2:
            return diag_a[DIAG.index((i, j))]
        return diag_b[DIAG.index((i - 2, j - 2))]

    rotation_body(tiles, sign, 1 - flags_ref[1], rot_ref, gen, gen_low, middle)


def rotation_mixed(flags, rot_b, diag_a, diag_b, sums, name):
    return pl.pallas_call(
        rotation_mixed_kernel,
        out_shape=struct((2, WIDE, HALF), BF16),
        in_specs=[SMEM] + [VMEM] * 7,
        out_specs=VMEM,
        scratch_shapes=ROTATION_SCRATCH
        + [pltpu.VMEM((2, 2, 128, WIDE), BF16), pltpu.VMEM((2, TILE, HALF), F32)],
        compiler_params=params(),
        cost_estimate=cost(2 * WIDE**3 + WIDE**3 // 4, 6 * 2**20),
        name=name,
    )(flags, rot_b, diag_a, diag_b, *sums)


CHUNK = 256


def half_kernel(half_ref, cols_ref, rot_ref, out_ref):
    half = half_ref[0]
    for k in range(ROWS // CHUNK):
        at = pl.ds(k * CHUNK, CHUNK)
        out = jnp.dot(cols_ref[at, :], rot_ref[half], preferred_element_type=F32)
        out_ref[at, :] = out.astype(BF16)


def apply_half(half, cols, rot, name):
    return pl.pallas_call(
        half_kernel,
        out_shape=struct((ROWS, HALF), BF16),
        in_specs=[SMEM, VMEM, VMEM],
        out_specs=VMEM,
        compiler_params=params(),
        cost_estimate=cost(ROWS * WIDE * HALF, ROWS * WIDE * 3 + 2**20),
        name=name,
    )(half, cols, rot)


def both_kernel(first_ref, second_ref, rot_ref, out_ref):
    for k in range(ROWS // CHUNK):
        at = pl.ds(k * CHUNK, CHUNK)
        cols = jnp.concatenate([first_ref[at, :], second_ref[at, :]], axis=1)
        for half in range(2):
            out = jnp.dot(cols, rot_ref[half], preferred_element_type=F32)
            out_ref[at, half * HALF : (half + 1) * HALF] = out.astype(BF16)


def apply_both(first, second, rot, name):
    return pl.pallas_call(
        both_kernel,
        out_shape=struct((ROWS, WIDE), BF16),
        in_specs=[VMEM] * 3,
        out_specs=VMEM,
        compiler_params=params(),
        cost_estimate=cost(ROWS * WIDE * WIDE, 2 * ROWS * WIDE * 2 + 2**21),
        name=name,
    )(first, second, rot)


def exchange(parts):
    return lax.all_to_all(parts, NODE_AXES, 0, 0, tiled=True)


def local(weight):
    core = lax.axis_index("core").astype(jnp.int32)
    node = jnp.asarray(np.array(NODE_AT, np.int32))[lax.axis_index(NODE_AXES)]
    core1 = core[None]

    def flags(first_is_upper, half=0):
        return jnp.stack([core, jnp.asarray(first_is_upper, jnp.int32), jnp.asarray(half, jnp.int32)])

    half_a = jnp.where(2 * node <= 16, 0, 1).astype(jnp.int32)
    half_b = jnp.where(2 * node + 1 <= 16, 1, 0).astype(jnp.int32)

    sent_a, sent_b = spread(weight)
    cols_a = exchange(sent_a).reshape(ROWS, WIDE)
    cols_b = exchange(sent_b).reshape(ROWS, WIDE)
    sums, _ = total(*gram(core1, (cols_a,), cols_a, "gram_a"))
    rot_a, diag_a = rotation_diag(flags(1, half_a), sums, "rotation_a")
    prev_a = apply_half(1 - half_a[None], cols_a, rot_a, "apply_a_prev")
    far_a = permute(prev_a, RING_BACK)
    in_a = apply_half(half_a[None], cols_a, rot_a, "apply_a_in")

    sums_b, _ = total(*gram(core1, (cols_b,), sums[1], "gram_b"))
    sums_mixed, midway = total(*mixed(core1, in_a, cols_b, "mixed"))
    rot_b, diag_b = rotation_diag(flags(1, half_b), sums_b, "rotation_b")
    in_b = apply_half(half_b[None], cols_b, rot_b, "apply_b_in")
    next_b = apply_half(1 - half_b[None], cols_b, rot_b, "apply_b_next")

    rot = rotation_mixed(
        flags(2 * node <= 15, half_b), rot_b, diag_a, diag_b, sums_mixed, "rotation_in"
    )
    parts = apply_both(in_a, in_b, rot, "apply_in").reshape(NODES, PER, WIDE)
    parts_in = exchange(parts)

    sums, _ = total(*gram(core1, (next_b, far_a), midway, "gram_off"))
    rot = rotation(flags(2 * node + 1 <= 15), sums, "rotation_off")
    parts = apply_both(next_b, far_a, rot, "apply_off").reshape(NODES, PER, WIDE)
    parts_off = exchange(parts)

    return gather(parts_off, 1, gather(parts_in, 0, None, "gather_in"), "gather_off")


def solution(mesh):
    fine = Mesh(mesh.devices.reshape(4, 2, 4, 2, 2), AXES)
    return jax.shard_map(
        local,
        mesh=fine,
        in_specs=(P(AXES, None),),
        out_specs=P(AXES, None),
        check_vma=False,
    )
```

```python
import jax
import jax.numpy as jnp
import numpy as np
from jax import lax
from jax.experimental import pallas as pl
from jax.experimental.pallas import tpu as pltpu
from jax.sharding import Mesh
from jax.sharding import PartitionSpec as P

NODES = 16
HALF = 512
WIDE = 1024
TILE = 256
PER = 64
ROWS = NODES * PER
AXES = ("x", "zh", "y", "zl", "core")
NODE_AXES = ("x", "y")
F32 = jnp.float32
BF16 = jnp.bfloat16
VMEM = pl.BlockSpec(memory_space=pltpu.VMEM)
SMEM = pl.BlockSpec(memory_space=pltpu.SMEM)
HBM = pl.BlockSpec(memory_space=pl.ANY)

RING = [0] + list(range(1, 32, 2)) + list(range(30, 0, -2))


def node_places():
    places = []
    for x in range(4):
        places += [x * 4 + (y if x % 2 == 0 else 3 - y) for y in range(4)]
    return places


PLACE = node_places()
NODE_AT = [PLACE.index(n) for n in range(NODES)]


def edge_pair(edge):
    return 2 * edge if edge <= 15 else 63 - 2 * edge


def flat(place, z, core):
    x, y = divmod(place, 4)
    zh, zl = divmod(z, 2)
    return (((x * 2 + zh) * 4 + y) * 2 + zl) * 2 + core


def all_perm(target):
    return [
        (flat(PLACE[j], z, c), flat(*target(j, z, c)))
        for j in range(NODES)
        for z in range(4)
        for c in range(2)
    ]


CORE_SWAP = all_perm(lambda j, z, c: (PLACE[j], z, 1 - c))
Z_EVEN = all_perm(lambda j, z, c: (PLACE[j], z ^ 1, c))
Z_ODD = all_perm(lambda j, z, c: (PLACE[j], 3 - z, c))
RING_BACK = all_perm(lambda j, z, c: (PLACE[(j - 1) % NODES], z, c))


def permute(value, table):
    return lax.ppermute(value, AXES, table)


def params(mebibytes=40):
    return pltpu.CompilerParams(vmem_limit_bytes=mebibytes * 1024 * 1024)


def cost(macs, nbytes):
    return pl.CostEstimate(flops=2 * macs, bytes_accessed=nbytes, transcendentals=0)


def struct(shape, dtype):
    return jax.ShapeDtypeStruct(shape, dtype)


def gram_dot(left, right):
    return lax.dot_general(left, right, (((0,), (0,)), ((), ())), preferred_element_type=F32)


GROUP = 4


def spread_kernel(weight_ref, *refs):
    outs, (held, load_sems, store_sems) = refs[:2], refs[2:]
    loads, stores = [], []
    for first, out_ref in enumerate(outs):
        for n in range(NODES):
            pair, place = RING[2 * NODE_AT[n] + first], first * NODES + n
            columns = weight_ref.at[:, pl.ds(pair * WIDE, WIDE)]
            loads.append(pltpu.make_async_copy(columns, held.at[place], load_sems.at[place]))
        for k in range(0, NODES, GROUP):
            place = first * NODES + k
            source, target = held.at[pl.ds(place, GROUP)], out_ref.at[pl.ds(k, GROUP)]
            stores.append(pltpu.make_async_copy(source, target, store_sems.at[place]))
    for load in loads:
        load.start()
    for k, store in enumerate(stores):
        for load in loads[GROUP * k : GROUP * (k + 1)]:
            load.wait()
        store.start()
    for store in stores:
        store.wait()


def spread(weight):
    out = struct((NODES, PER, WIDE), BF16)
    return pl.pallas_call(
        spread_kernel,
        out_shape=(out, out),
        in_specs=[HBM],
        out_specs=(HBM, HBM),
        scratch_shapes=[
            pltpu.VMEM((2 * NODES, PER, WIDE), BF16),
            pltpu.SemaphoreType.DMA((2 * NODES,)),
            pltpu.SemaphoreType.DMA((2 * NODES,)),
        ],
        compiler_params=params(60),
        cost_estimate=cost(0, 4 * ROWS * WIDE * 2),
        name="spread",
    )(weight)


def gather(parts, first, whole, name):
    def kernel(parts_ref, *refs):
        out_ref, sems = refs[-2:]
        stores = []
        for n in range(NODES):
            pair = edge_pair(2 * NODE_AT[n] + first)
            columns = out_ref.at[:, pl.ds(pair * WIDE, WIDE)]
            stores.append(pltpu.make_async_copy(parts_ref.at[n], columns, sems.at[n]))
        for store in stores:
            store.start()
        for store in stores:
            store.wait()

    operands = (parts,) if whole is None else (parts, whole)
    return pl.pallas_call(
        kernel,
        out_shape=struct((PER, 2 * NODES * WIDE), BF16),
        in_specs=[VMEM, HBM][: len(operands)],
        out_specs=HBM,
        scratch_shapes=[pltpu.SemaphoreType.DMA((NODES,))],
        input_output_aliases={} if whole is None else {1: 0},
        compiler_params=params(),
        cost_estimate=cost(0, 2 * ROWS * WIDE * 2),
        name=name,
    )(*operands)


TILES = [(0, 0), (0, 1), (1, 1), (0, 2), (0, 3), (2, 2), (2, 3), (3, 3), (1, 2), (1, 3)]


def gram_body(core, first, second, mine_ref, other_ref):
    def put(row, col, tile):
        owner, slot = divmod(TILES.index((row, col)), 5)
        for half in range(2):
            part = tile[half * 128 : (half + 1) * 128]

            @pl.when(core == owner)
            def _():
                mine_ref[2 * slot + half] = part

            @pl.when(core != owner)
            def _():
                other_ref[2 * slot + half] = part.astype(BF16)

    for block, cols in ((0, first), (2, second)):
        for i in range(2):
            left = cols[:, i * TILE : (i + 1) * TILE]
            strip = gram_dot(left, cols[:, i * TILE :])
            for j in range(i, 2):
                put(block + i, block + j, strip[:, (j - i) * TILE : (j - i + 1) * TILE])
            if block == 0:
                strip = gram_dot(left, second[...])
                for j in range(2):
                    put(i, 2 + j, strip[:, j * TILE : (j + 1) * TILE])


def gram_whole_kernel(core_ref, cols_ref, after_ref, mine_ref, other_ref):
    first, second = cols_ref.at[:, pl.ds(0, HALF)], cols_ref.at[:, pl.ds(HALF, HALF)]
    gram_body(core_ref[0], first, second, mine_ref, other_ref)


def gram_halves_kernel(core_ref, first_ref, second_ref, after_ref, mine_ref, other_ref):
    gram_body(core_ref[0], first_ref, second_ref, mine_ref, other_ref)


def gram(core, cols, after, name):
    return pl.pallas_call(
        gram_whole_kernel if len(cols) == 1 else gram_halves_kernel,
        out_shape=(struct((10, 128, TILE), F32), struct((10, 128, TILE), BF16)),
        in_specs=[SMEM] + [VMEM] * len(cols) + [HBM],
        out_specs=(VMEM, VMEM),
        compiler_params=params(),
        cost_estimate=cost(10 * ROWS * TILE * TILE, ROWS * WIDE * 2 + 2**21),
        name=name,
    )(core, *cols, after)


def mixed_kernel(core_ref, done_ref, cols_ref, mine_ref, other_ref):
    for i in range(2):
        strip = gram_dot(done_ref[:, i * TILE : (i + 1) * TILE], cols_ref[...])
        for half in range(2):
            part = strip[half * 128 : (half + 1) * 128]

            @pl.when(core_ref[0] == i)
            def _():
                mine_ref[half] = part

            @pl.when(core_ref[0] != i)
            def _():
                other_ref[half] = part.astype(BF16)


def mixed(core, done, cols, name):
    return pl.pallas_call(
        mixed_kernel,
        out_shape=(struct((2, 128, WIDE), F32), struct((2, 128, WIDE), BF16)),
        in_specs=[SMEM, VMEM, VMEM],
        out_specs=(VMEM, VMEM),
        compiler_params=params(),
        cost_estimate=cost(ROWS * HALF * WIDE, ROWS * WIDE * 3 + 2**21),
        name=name,
    )(core, done, cols)


def add(left, right):
    return (left.astype(F32) + right.astype(F32)).astype(BF16)


def total(mine, other):
    far = permute(other, CORE_SWAP)
    cut = other.shape[0] // 2
    low, high = add(mine[:cut], far[:cut]), add(mine[cut:], far[cut:])
    low, high = add(low, permute(low, Z_EVEN)), add(high, permute(high, Z_ODD))
    low, high = add(low, permute(low, Z_ODD)), add(high, permute(high, Z_EVEN))
    return low, high, permute(low, CORE_SWAP), permute(high, CORE_SWAP)


def rotation_body(tiles, sign, slot, rot_ref, gen, gen_low, middle):
    rows = lax.broadcasted_iota(jnp.int32, (TILE, TILE), 0)
    cols = lax.broadcasted_iota(jnp.int32, (TILE, TILE), 1)
    down, across = [], []
    for i in range(4):
        only = jnp.where(rows == cols, tiles(i, i), 0.0)
        down.append(jnp.sum(only, axis=1, keepdims=True))
        across.append(jnp.sum(only, axis=0, keepdims=True))
    total = jnp.zeros((TILE, TILE), F32)
    for i in range(4):
        for j in range(i, 4):
            upper = tiles(i, j) / (down[i] + across[j] + 0.001)
            if i == j:
                upper = jnp.where(rows < cols, upper, 0.0)
            elif i < 2 <= j:
                upper = upper * sign
            total = total + upper * upper
            at_i, at_j = pl.ds(i * TILE, TILE), pl.ds(j * TILE, TILE)
            if i == j:
                both = upper - upper.T
                gen[at_i, at_j] = both
                gen_low[at_i, at_j] = both.astype(BF16)
            else:
                flipped = -upper.T
                gen[at_i, at_j] = upper
                gen_low[at_i, at_j] = upper.astype(BF16)
                gen[at_j, at_i] = flipped
                gen_low[at_j, at_i] = flipped.astype(BF16)
    norm_sq = 1.0 + 2.0 * jnp.sum(total, keepdims=True) / WIDE
    inv_norm = lax.rsqrt(norm_sq)
    scale = 0.5 * inv_norm * inv_norm
    wide_rows = lax.broadcasted_iota(jnp.int32, (TILE, WIDE), 0)
    wide_cols = lax.broadcasted_iota(jnp.int32, (TILE, WIDE), 1)
    for i in range(4):
        at = pl.ds(i * TILE, TILE)
        squared = jnp.dot(gen_low[at, :], gen_low[...], preferred_element_type=F32)
        identity = jnp.where(wide_rows + i * TILE == wide_cols, 1.0, 0.0)
        middle[at, :] = (1.5 * identity - scale * (identity - squared)).astype(BF16)
    for i in range(4):
        at = pl.ds(i * TILE, TILE)
        identity = jnp.where(wide_rows + i * TILE == wide_cols, 1.0, 0.0)
        start_rot = ((identity + gen[at, :]) * inv_norm).astype(BF16)
        strip = jnp.dot(start_rot, middle[...], preferred_element_type=F32).astype(BF16)
        rot_ref[slot, at, :] = strip[:, :HALF]
        rot_ref[1 - slot, at, :] = strip[:, HALF:]


ROTATION_SCRATCH = [
    pltpu.VMEM((WIDE, WIDE), F32),
    pltpu.VMEM((WIDE, WIDE), BF16),
    pltpu.VMEM((WIDE, WIDE), BF16),
]


def hold(core, sums, held):
    own_low, own_high, far_low, far_high = sums
    cut = own_low.shape[0]
    held[core, :cut] = own_low[...]
    held[core, cut:] = own_high[...]
    held[1 - core, :cut] = far_low[...]
    held[1 - core, cut:] = far_high[...]


def held_tile(held, i, j):
    owner, slot = divmod(TILES.index((i, j)), 5)
    return held[owner, 2 * slot : 2 * slot + 2].reshape(TILE, TILE)


HELD = [pltpu.VMEM((2, 10, 128, TILE), BF16)]
DIAG = [(0, 0), (0, 1), (1, 1)]


def rotation_kernel(flags_ref, *refs):
    rot_ref, gen, gen_low, middle, held = refs[4:]
    hold(flags_ref[0], refs[:4], held)
    sign = jnp.where(flags_ref[1] == 1, 1.0, -1.0)

    def tiles(i, j):
        return held_tile(held, i, j).astype(F32)

    rotation_body(tiles, sign, 1 - flags_ref[1], rot_ref, gen, gen_low, middle)


def rotation(flags, sums, name):
    return pl.pallas_call(
        rotation_kernel,
        out_shape=struct((2, WIDE, HALF), BF16),
        in_specs=[SMEM] + [VMEM] * 4,
        out_specs=VMEM,
        scratch_shapes=ROTATION_SCRATCH + HELD,
        compiler_params=params(),
        cost_estimate=cost(2 * WIDE**3, 4 * 2**20),
        name=name,
    )(flags, *sums)


def rotation_diag_kernel(flags_ref, *refs):
    rot_ref, diag_ref, gen, gen_low, middle, held, gram_all, turned = refs[4:]
    hold(flags_ref[0], refs[:4], held)

    def tiles(i, j):
        return held_tile(held, i, j).astype(F32)

    rotation_body(tiles, 1.0, 0, rot_ref, gen, gen_low, middle)
    for i in range(4):
        for j in range(i, 4):
            at_i, at_j = pl.ds(i * TILE, TILE), pl.ds(j * TILE, TILE)
            tile = held_tile(held, i, j)
            gram_all[at_i, at_j] = tile
            if i != j:
                gram_all[at_j, at_i] = tile.astype(F32).T.astype(BF16)
    rot = rot_ref.at[flags_ref[2]]
    for i in range(4):
        at = pl.ds(i * TILE, TILE)
        turned[at, :] = jnp.dot(gram_all[at, :], rot[...], preferred_element_type=F32).astype(BF16)
    for place, (i, j) in enumerate(DIAG):
        at_i, at_j = pl.ds(i * TILE, TILE), pl.ds(j * TILE, TILE)
        diag_ref[place] = gram_dot(rot[:, at_i], turned[:, at_j])


def rotation_diag(flags, sums, name):
    return pl.pallas_call(
        rotation_diag_kernel,
        out_shape=(struct((2, WIDE, HALF), BF16), struct((3, TILE, TILE), F32)),
        in_specs=[SMEM] + [VMEM] * 4,
        out_specs=(VMEM, VMEM),
        scratch_shapes=ROTATION_SCRATCH
        + HELD
        + [pltpu.VMEM((WIDE, WIDE), BF16), pltpu.VMEM((WIDE, HALF), BF16)],
        compiler_params=params(),
        cost_estimate=cost(3 * WIDE**3, 6 * 2**20),
        name=name,
    )(flags, *sums)


def rotation_mixed_kernel(flags_ref, rot_b, diag_a, diag_b, *refs):
    rot_ref, gen, gen_low, middle, held, cross = refs[4:]
    hold(flags_ref[0], refs[:4], held)
    sign = jnp.where(flags_ref[1] == 1, 1.0, -1.0)
    for i in range(2):
        strip = held[i].reshape(TILE, WIDE)
        cross[i] = jnp.dot(strip, rot_b[flags_ref[2]], preferred_element_type=F32)

    def tiles(i, j):
        if i < 2 <= j:
            return cross[i, :, (j - 2) * TILE : (j - 1) * TILE]
        if j < 2:
            return diag_a[DIAG.index((i, j))]
        return diag_b[DIAG.index((i - 2, j - 2))]

    rotation_body(tiles, sign, 1 - flags_ref[1], rot_ref, gen, gen_low, middle)


def rotation_mixed(flags, rot_b, diag_a, diag_b, sums, name):
    return pl.pallas_call(
        rotation_mixed_kernel,
        out_shape=struct((2, WIDE, HALF), BF16),
        in_specs=[SMEM] + [VMEM] * 7,
        out_specs=VMEM,
        scratch_shapes=ROTATION_SCRATCH
        + [pltpu.VMEM((2, 2, 128, WIDE), BF16), pltpu.VMEM((2, TILE, HALF), F32)],
        compiler_params=params(),
        cost_estimate=cost(2 * WIDE**3 + WIDE**3 // 4, 6 * 2**20),
        name=name,
    )(flags, rot_b, diag_a, diag_b, *sums)


CHUNK = 256


def half_kernel(half_ref, cols_ref, rot_ref, out_ref):
    half = half_ref[0]
    for k in range(ROWS // CHUNK):
        at = pl.ds(k * CHUNK, CHUNK)
        out = jnp.dot(cols_ref[at, :], rot_ref[half], preferred_element_type=F32)
        out_ref[at, :] = out.astype(BF16)


def apply_half(half, cols, rot, name):
    return pl.pallas_call(
        half_kernel,
        out_shape=struct((ROWS, HALF), BF16),
        in_specs=[SMEM, VMEM, VMEM],
        out_specs=VMEM,
        compiler_params=params(),
        cost_estimate=cost(ROWS * WIDE * HALF, ROWS * WIDE * 3 + 2**20),
        name=name,
    )(half, cols, rot)


def both_kernel(first_ref, second_ref, rot_ref, out_ref):
    for k in range(ROWS // CHUNK):
        at = pl.ds(k * CHUNK, CHUNK)
        cols = jnp.concatenate([first_ref[at, :], second_ref[at, :]], axis=1)
        for half in range(2):
            out = jnp.dot(cols, rot_ref[half], preferred_element_type=F32)
            out_ref[at, half * HALF : (half + 1) * HALF] = out.astype(BF16)


def apply_both(first, second, rot, name):
    return pl.pallas_call(
        both_kernel,
        out_shape=struct((ROWS, WIDE), BF16),
        in_specs=[VMEM] * 3,
        out_specs=VMEM,
        compiler_params=params(),
        cost_estimate=cost(ROWS * WIDE * WIDE, 2 * ROWS * WIDE * 2 + 2**21),
        name=name,
    )(first, second, rot)


def exchange(parts):
    return lax.all_to_all(parts, NODE_AXES, 0, 0, tiled=True)


def local(weight):
    core = lax.axis_index("core").astype(jnp.int32)
    node = jnp.asarray(np.array(NODE_AT, np.int32))[lax.axis_index(NODE_AXES)]
    core1 = core[None]

    def flags(first_is_upper, half=0):
        return jnp.stack([core, jnp.asarray(first_is_upper, jnp.int32), jnp.asarray(half, jnp.int32)])

    half_a = jnp.where(2 * node <= 16, 0, 1).astype(jnp.int32)
    half_b = jnp.where(2 * node + 1 <= 16, 1, 0).astype(jnp.int32)

    sent_a, sent_b = spread(weight)
    cols_a = exchange(sent_a).reshape(ROWS, WIDE)
    cols_b = exchange(sent_b).reshape(ROWS, WIDE)
    sums = total(*gram(core1, (cols_a,), cols_a, "gram_a"))
    rot_a, diag_a = rotation_diag(flags(1, half_a), sums, "rotation_a")
    prev_a = apply_half(1 - half_a[None], cols_a, rot_a, "apply_a_prev")
    far_a = permute(prev_a, RING_BACK)
    in_a = apply_half(half_a[None], cols_a, rot_a, "apply_a_in")

    sums_b = total(*gram(core1, (cols_b,), sums[1], "gram_b"))
    sums_mixed = total(*mixed(core1, in_a, cols_b, "mixed"))
    rot_b, diag_b = rotation_diag(flags(1, half_b), sums_b, "rotation_b")
    in_b = apply_half(half_b[None], cols_b, rot_b, "apply_b_in")
    next_b = apply_half(1 - half_b[None], cols_b, rot_b, "apply_b_next")

    rot = rotation_mixed(
        flags(2 * node <= 15, half_b), rot_b, diag_a, diag_b, sums_mixed, "rotation_in"
    )
    parts = apply_both(in_a, in_b, rot, "apply_in").reshape(NODES, PER, WIDE)
    parts_in = exchange(parts)

    sums = total(*gram(core1, (next_b, far_a), sums_mixed[3], "gram_off"))
    rot = rotation(flags(2 * node + 1 <= 15), sums, "rotation_off")
    parts = apply_both(next_b, far_a, rot, "apply_off").reshape(NODES, PER, WIDE)
    parts_off = exchange(parts)

    return gather(parts_off, 1, gather(parts_in, 0, None, "gather_in"), "gather_off")


def solution(mesh):
    fine = Mesh(mesh.devices.reshape(4, 2, 4, 2, 2), AXES)
    return jax.shard_map(
        local,
        mesh=fine,
        in_specs=(P(AXES, None),),
        out_specs=P(AXES, None),
        check_vma=False,
    )
```

```python
import jax
import jax.numpy as jnp
import numpy as np
from jax import lax
from jax.experimental import pallas as pl
from jax.experimental.pallas import tpu as pltpu
from jax.sharding import Mesh
from jax.sharding import PartitionSpec as P

NODES = 16
HALF = 512
WIDE = 1024
TILE = 256
PER = 64
ROWS = NODES * PER
AXES = ("x", "zh", "y", "zl", "core")
NODE_AXES = ("x", "y")
F32 = jnp.float32
BF16 = jnp.bfloat16
VMEM = pl.BlockSpec(memory_space=pltpu.VMEM)
SMEM = pl.BlockSpec(memory_space=pltpu.SMEM)
HBM = pl.BlockSpec(memory_space=pl.ANY)

RING = [0] + list(range(1, 32, 2)) + list(range(30, 0, -2))


def node_places():
    places = []
    for x in range(4):
        places += [x * 4 + (y if x % 2 == 0 else 3 - y) for y in range(4)]
    return places


PLACE = node_places()
NODE_AT = [PLACE.index(n) for n in range(NODES)]


def edge_pair(edge):
    return 2 * edge if edge <= 15 else 63 - 2 * edge


def flat(place, z, core):
    x, y = divmod(place, 4)
    zh, zl = divmod(z, 2)
    return (((x * 2 + zh) * 4 + y) * 2 + zl) * 2 + core


def all_perm(target):
    return [
        (flat(PLACE[j], z, c), flat(*target(j, z, c)))
        for j in range(NODES)
        for z in range(4)
        for c in range(2)
    ]


CORE_SWAP = all_perm(lambda j, z, c: (PLACE[j], z, 1 - c))
Z_EVEN = all_perm(lambda j, z, c: (PLACE[j], z ^ 1, c))
Z_ODD = all_perm(lambda j, z, c: (PLACE[j], 3 - z, c))
RING_BACK = all_perm(lambda j, z, c: (PLACE[(j - 1) % NODES], z, c))


def permute(value, table):
    return lax.ppermute(value, AXES, table)


def params(mebibytes=40):
    return pltpu.CompilerParams(vmem_limit_bytes=mebibytes * 1024 * 1024)


def cost(macs, nbytes):
    return pl.CostEstimate(flops=2 * macs, bytes_accessed=nbytes, transcendentals=0)


def struct(shape, dtype):
    return jax.ShapeDtypeStruct(shape, dtype)


def gram_dot(left, right):
    return lax.dot_general(left, right, (((0,), (0,)), ((), ())), preferred_element_type=F32)


GROUP = 4


def spread_kernel(weight_ref, *refs):
    outs, (held, load_sems, store_sems) = refs[:2], refs[2:]
    loads, stores = [], []
    for first, out_ref in enumerate(outs):
        for n in range(NODES):
            pair, place = RING[2 * NODE_AT[n] + first], first * NODES + n
            columns = weight_ref.at[:, pl.ds(pair * WIDE, WIDE)]
            loads.append(pltpu.make_async_copy(columns, held.at[place], load_sems.at[place]))
        for k in range(0, NODES, GROUP):
            place = first * NODES + k
            source, target = held.at[pl.ds(place, GROUP)], out_ref.at[pl.ds(k, GROUP)]
            stores.append(pltpu.make_async_copy(source, target, store_sems.at[place]))
    for load in loads:
        load.start()
    for k, store in enumerate(stores):
        for load in loads[GROUP * k : GROUP * (k + 1)]:
            load.wait()
        store.start()
    for store in stores:
        store.wait()


def spread(weight):
    out = struct((NODES, PER, WIDE), BF16)
    return pl.pallas_call(
        spread_kernel,
        out_shape=(out, out),
        in_specs=[HBM],
        out_specs=(HBM, HBM),
        scratch_shapes=[
            pltpu.VMEM((2 * NODES, PER, WIDE), BF16),
            pltpu.SemaphoreType.DMA((2 * NODES,)),
            pltpu.SemaphoreType.DMA((2 * NODES,)),
        ],
        compiler_params=params(60),
        cost_estimate=cost(0, 4 * ROWS * WIDE * 2),
        name="spread",
    )(weight)


def gather(parts, first, whole, name):
    def kernel(parts_ref, *refs):
        out_ref, sems = refs[-2:]
        stores = []
        for n in range(NODES):
            pair = edge_pair(2 * NODE_AT[n] + first)
            columns = out_ref.at[:, pl.ds(pair * WIDE, WIDE)]
            stores.append(pltpu.make_async_copy(parts_ref.at[n], columns, sems.at[n]))
        for store in stores:
            store.start()
        for store in stores:
            store.wait()

    operands = (parts,) if whole is None else (parts, whole)
    return pl.pallas_call(
        kernel,
        out_shape=struct((PER, 2 * NODES * WIDE), BF16),
        in_specs=[VMEM, HBM][: len(operands)],
        out_specs=HBM,
        scratch_shapes=[pltpu.SemaphoreType.DMA((NODES,))],
        input_output_aliases={} if whole is None else {1: 0},
        compiler_params=params(),
        cost_estimate=cost(0, 2 * ROWS * WIDE * 2),
        name=name,
    )(*operands)


TILES = [(0, 0), (0, 1), (1, 1), (0, 2), (0, 3), (2, 2), (2, 3), (3, 3), (1, 2), (1, 3)]


def gram_body(core, first, second, mine_ref, other_ref):
    def put(row, col, tile):
        owner, slot = divmod(TILES.index((row, col)), 5)
        for half in range(2):
            part = tile[half * 128 : (half + 1) * 128]

            @pl.when(core == owner)
            def _():
                mine_ref[2 * slot + half] = part

            @pl.when(core != owner)
            def _():
                other_ref[2 * slot + half] = part.astype(BF16)

    for block, cols in ((0, first), (2, second)):
        for i in range(2):
            left = cols[:, i * TILE : (i + 1) * TILE]
            strip = gram_dot(left, cols[:, i * TILE :])
            for j in range(i, 2):
                put(block + i, block + j, strip[:, (j - i) * TILE : (j - i + 1) * TILE])
            if block == 0:
                strip = gram_dot(left, second[...])
                for j in range(2):
                    put(i, 2 + j, strip[:, j * TILE : (j + 1) * TILE])


def gram_whole_kernel(core_ref, cols_ref, after_ref, mine_ref, other_ref):
    first, second = cols_ref.at[:, pl.ds(0, HALF)], cols_ref.at[:, pl.ds(HALF, HALF)]
    gram_body(core_ref[0], first, second, mine_ref, other_ref)


def gram_halves_kernel(core_ref, first_ref, second_ref, after_ref, mine_ref, other_ref):
    gram_body(core_ref[0], first_ref, second_ref, mine_ref, other_ref)


def gram(core, cols, after, name):
    return pl.pallas_call(
        gram_whole_kernel if len(cols) == 1 else gram_halves_kernel,
        out_shape=(struct((10, 128, TILE), F32), struct((10, 128, TILE), BF16)),
        in_specs=[SMEM] + [VMEM] * len(cols) + [HBM],
        out_specs=(VMEM, VMEM),
        compiler_params=params(),
        cost_estimate=cost(10 * ROWS * TILE * TILE, ROWS * WIDE * 2 + 2**21),
        name=name,
    )(core, *cols, after)


def mixed_kernel(core_ref, done_ref, cols_ref, mine_ref, other_ref):
    for i in range(2):
        strip = gram_dot(done_ref[:, i * TILE : (i + 1) * TILE], cols_ref[...])
        for half in range(2):
            part = strip[half * 128 : (half + 1) * 128]

            @pl.when(core_ref[0] == i)
            def _():
                mine_ref[half] = part

            @pl.when(core_ref[0] != i)
            def _():
                other_ref[half] = part.astype(BF16)


def mixed(core, done, cols, name):
    return pl.pallas_call(
        mixed_kernel,
        out_shape=(struct((2, 128, WIDE), F32), struct((2, 128, WIDE), BF16)),
        in_specs=[SMEM, VMEM, VMEM],
        out_specs=(VMEM, VMEM),
        compiler_params=params(),
        cost_estimate=cost(ROWS * HALF * WIDE, ROWS * WIDE * 3 + 2**21),
        name=name,
    )(core, done, cols)


def add(left, right):
    return (left.astype(F32) + right.astype(F32)).astype(BF16)


def total(mine, other):
    far = permute(other, CORE_SWAP)
    cut = other.shape[0] // 2
    low, high = add(mine[:cut], far[:cut]), add(mine[cut:], far[cut:])
    midway, high = add(low, permute(low, Z_EVEN)), add(high, permute(high, Z_ODD))
    low, high = add(midway, permute(midway, Z_ODD)), add(high, permute(high, Z_EVEN))
    return (low, high, permute(low, CORE_SWAP), permute(high, CORE_SWAP)), midway


def rotation_body(tiles, sign, slot, rot_ref, gen, gen_low, middle):
    rows = lax.broadcasted_iota(jnp.int32, (TILE, TILE), 0)
    cols = lax.broadcasted_iota(jnp.int32, (TILE, TILE), 1)
    down, across = [], []
    for i in range(4):
        only = jnp.where(rows == cols, tiles(i, i), 0.0)
        down.append(jnp.sum(only, axis=1, keepdims=True))
        across.append(jnp.sum(only, axis=0, keepdims=True))
    total = jnp.zeros((TILE, TILE), F32)
    for i in range(4):
        for j in range(i, 4):
            upper = tiles(i, j) / (down[i] + across[j] + 0.001)
            if i == j:
                upper = jnp.where(rows < cols, upper, 0.0)
            elif i < 2 <= j:
                upper = upper * sign
            total = total + upper * upper
            at_i, at_j = pl.ds(i * TILE, TILE), pl.ds(j * TILE, TILE)
            if i == j:
                both = upper - upper.T
                gen[at_i, at_j] = both
                gen_low[at_i, at_j] = both.astype(BF16)
            else:
                flipped = -upper.T
                gen[at_i, at_j] = upper
                gen_low[at_i, at_j] = upper.astype(BF16)
                gen[at_j, at_i] = flipped
                gen_low[at_j, at_i] = flipped.astype(BF16)
    norm_sq = 1.0 + 2.0 * jnp.sum(total, keepdims=True) / WIDE
    inv_norm = lax.rsqrt(norm_sq)
    scale = 0.5 * inv_norm * inv_norm
    wide_rows = lax.broadcasted_iota(jnp.int32, (TILE, WIDE), 0)
    wide_cols = lax.broadcasted_iota(jnp.int32, (TILE, WIDE), 1)
    for i in range(4):
        at = pl.ds(i * TILE, TILE)
        squared = jnp.dot(gen_low[at, :], gen_low[...], preferred_element_type=F32)
        identity = jnp.where(wide_rows + i * TILE == wide_cols, 1.0, 0.0)
        middle[at, :] = (1.5 * identity - scale * (identity - squared)).astype(BF16)
    for i in range(4):
        at = pl.ds(i * TILE, TILE)
        identity = jnp.where(wide_rows + i * TILE == wide_cols, 1.0, 0.0)
        start_rot = ((identity + gen[at, :]) * inv_norm).astype(BF16)
        strip = jnp.dot(start_rot, middle[...], preferred_element_type=F32).astype(BF16)
        rot_ref[slot, at, :] = strip[:, :HALF]
        rot_ref[1 - slot, at, :] = strip[:, HALF:]


ROTATION_SCRATCH = [
    pltpu.VMEM((WIDE, WIDE), F32),
    pltpu.VMEM((WIDE, WIDE), BF16),
    pltpu.VMEM((WIDE, WIDE), BF16),
]


def hold(core, sums, held):
    own_low, own_high, far_low, far_high = sums
    cut = own_low.shape[0]
    held[core, :cut] = own_low[...]
    held[core, cut:] = own_high[...]
    held[1 - core, :cut] = far_low[...]
    held[1 - core, cut:] = far_high[...]


def held_tile(held, i, j):
    owner, slot = divmod(TILES.index((i, j)), 5)
    return held[owner, 2 * slot : 2 * slot + 2].reshape(TILE, TILE)


HELD = [pltpu.VMEM((2, 10, 128, TILE), BF16)]
DIAG = [(0, 0), (0, 1), (1, 1)]


def rotation_kernel(flags_ref, *refs):
    rot_ref, gen, gen_low, middle, held = refs[4:]
    hold(flags_ref[0], refs[:4], held)
    sign = jnp.where(flags_ref[1] == 1, 1.0, -1.0)

    def tiles(i, j):
        return held_tile(held, i, j).astype(F32)

    rotation_body(tiles, sign, 1 - flags_ref[1], rot_ref, gen, gen_low, middle)


def rotation(flags, sums, name):
    return pl.pallas_call(
        rotation_kernel,
        out_shape=struct((2, WIDE, HALF), BF16),
        in_specs=[SMEM] + [VMEM] * 4,
        out_specs=VMEM,
        scratch_shapes=ROTATION_SCRATCH + HELD,
        compiler_params=params(),
        cost_estimate=cost(2 * WIDE**3, 4 * 2**20),
        name=name,
    )(flags, *sums)


def rotation_diag_kernel(flags_ref, *refs):
    rot_ref, diag_ref, gen, gen_low, middle, held, gram_all, turned = refs[4:]
    hold(flags_ref[0], refs[:4], held)

    def tiles(i, j):
        return held_tile(held, i, j).astype(F32)

    rotation_body(tiles, 1.0, 0, rot_ref, gen, gen_low, middle)
    for i in range(4):
        for j in range(i, 4):
            at_i, at_j = pl.ds(i * TILE, TILE), pl.ds(j * TILE, TILE)
            tile = held_tile(held, i, j)
            gram_all[at_i, at_j] = tile
            if i != j:
                gram_all[at_j, at_i] = tile.astype(F32).T.astype(BF16)
    rot = rot_ref.at[flags_ref[2]]
    for i in range(4):
        at = pl.ds(i * TILE, TILE)
        turned[at, :] = jnp.dot(gram_all[at, :], rot[...], preferred_element_type=F32).astype(BF16)
    for place, (i, j) in enumerate(DIAG):
        at_i, at_j = pl.ds(i * TILE, TILE), pl.ds(j * TILE, TILE)
        diag_ref[place] = gram_dot(rot[:, at_i], turned[:, at_j])


def rotation_diag(flags, sums, name):
    return pl.pallas_call(
        rotation_diag_kernel,
        out_shape=(struct((2, WIDE, HALF), BF16), struct((3, TILE, TILE), F32)),
        in_specs=[SMEM] + [VMEM] * 4,
        out_specs=(VMEM, VMEM),
        scratch_shapes=ROTATION_SCRATCH
        + HELD
        + [pltpu.VMEM((WIDE, WIDE), BF16), pltpu.VMEM((WIDE, HALF), BF16)],
        compiler_params=params(),
        cost_estimate=cost(3 * WIDE**3, 6 * 2**20),
        name=name,
    )(flags, *sums)


def rotation_mixed_kernel(flags_ref, rot_b, diag_a, diag_b, *refs):
    rot_ref, gen, gen_low, middle, held, cross = refs[4:]
    hold(flags_ref[0], refs[:4], held)
    sign = jnp.where(flags_ref[1] == 1, 1.0, -1.0)
    for i in range(2):
        strip = held[i].reshape(TILE, WIDE)
        cross[i] = jnp.dot(strip, rot_b[flags_ref[2]], preferred_element_type=F32)

    def tiles(i, j):
        if i < 2 <= j:
            return cross[i, :, (j - 2) * TILE : (j - 1) * TILE]
        if j < 2:
            return diag_a[DIAG.index((i, j))]
        return diag_b[DIAG.index((i - 2, j - 2))]

    rotation_body(tiles, sign, 1 - flags_ref[1], rot_ref, gen, gen_low, middle)


def rotation_mixed(flags, rot_b, diag_a, diag_b, sums, name):
    return pl.pallas_call(
        rotation_mixed_kernel,
        out_shape=struct((2, WIDE, HALF), BF16),
        in_specs=[SMEM] + [VMEM] * 7,
        out_specs=VMEM,
        scratch_shapes=ROTATION_SCRATCH
        + [pltpu.VMEM((2, 2, 128, WIDE), BF16), pltpu.VMEM((2, TILE, HALF), F32)],
        compiler_params=params(),
        cost_estimate=cost(2 * WIDE**3 + WIDE**3 // 4, 6 * 2**20),
        name=name,
    )(flags, rot_b, diag_a, diag_b, *sums)


CHUNK = 256


def half_kernel(half_ref, cols_ref, rot_ref, out_ref):
    half = half_ref[0]
    for k in range(ROWS // CHUNK):
        at = pl.ds(k * CHUNK, CHUNK)
        out = jnp.dot(cols_ref[at, :], rot_ref[half], preferred_element_type=F32)
        out_ref[at, :] = out.astype(BF16)


def apply_half(half, cols, rot, name):
    return pl.pallas_call(
        half_kernel,
        out_shape=struct((ROWS, HALF), BF16),
        in_specs=[SMEM, VMEM, VMEM],
        out_specs=VMEM,
        compiler_params=params(),
        cost_estimate=cost(ROWS * WIDE * HALF, ROWS * WIDE * 3 + 2**20),
        name=name,
    )(half, cols, rot)


def both_kernel(first_ref, second_ref, rot_ref, out_ref):
    for k in range(ROWS // CHUNK):
        at = pl.ds(k * CHUNK, CHUNK)
        cols = jnp.concatenate([first_ref[at, :], second_ref[at, :]], axis=1)
        for half in range(2):
            out = jnp.dot(cols, rot_ref[half], preferred_element_type=F32)
            out_ref[at, half * HALF : (half + 1) * HALF] = out.astype(BF16)


def apply_both(first, second, rot, name):
    return pl.pallas_call(
        both_kernel,
        out_shape=struct((ROWS, WIDE), BF16),
        in_specs=[VMEM] * 3,
        out_specs=VMEM,
        compiler_params=params(),
        cost_estimate=cost(ROWS * WIDE * WIDE, 2 * ROWS * WIDE * 2 + 2**21),
        name=name,
    )(first, second, rot)


def exchange(parts):
    return lax.all_to_all(parts, NODE_AXES, 0, 0, tiled=True)


def local(weight):
    core = lax.axis_index("core").astype(jnp.int32)
    node = jnp.asarray(np.array(NODE_AT, np.int32))[lax.axis_index(NODE_AXES)]
    core1 = core[None]

    def flags(first_is_upper, half=0):
        return jnp.stack([core, jnp.asarray(first_is_upper, jnp.int32), jnp.asarray(half, jnp.int32)])

    half_a = jnp.where(2 * node <= 16, 0, 1).astype(jnp.int32)
    half_b = jnp.where(2 * node + 1 <= 16, 1, 0).astype(jnp.int32)

    sent_a, sent_b = spread(weight)
    cols_a = exchange(sent_a).reshape(ROWS, WIDE)
    cols_b = exchange(sent_b).reshape(ROWS, WIDE)
    sums, _ = total(*gram(core1, (cols_a,), cols_a, "gram_a"))
    rot_a, diag_a = rotation_diag(flags(1, half_a), sums, "rotation_a")
    prev_a = apply_half(1 - half_a[None], cols_a, rot_a, "apply_a_prev")
    far_a = permute(prev_a, RING_BACK)
    in_a = apply_half(half_a[None], cols_a, rot_a, "apply_a_in")

    sums_b, _ = total(*gram(core1, (cols_b,), sums[1], "gram_b"))
    sums_mixed, midway = total(*mixed(core1, in_a, cols_b, "mixed"))
    rot_b, diag_b = rotation_diag(flags(1, half_b), sums_b, "rotation_b")
    in_b = apply_half(half_b[None], cols_b, rot_b, "apply_b_in")
    next_b = apply_half(1 - half_b[None], cols_b, rot_b, "apply_b_next")

    rot = rotation_mixed(
        flags(2 * node <= 15, half_b), rot_b, diag_a, diag_b, sums_mixed, "rotation_in"
    )
    parts = apply_both(in_a, in_b, rot, "apply_in").reshape(NODES, PER, WIDE)
    parts_in = exchange(parts)

    sums, _ = total(*gram(core1, (next_b, far_a), rot, "gram_off"))
    rot = rotation(flags(2 * node + 1 <= 15), sums, "rotation_off")
    parts = apply_both(next_b, far_a, rot, "apply_off").reshape(NODES, PER, WIDE)
    parts_off = exchange(parts)

    return gather(parts_off, 1, gather(parts_in, 0, None, "gather_in"), "gather_off")


def solution(mesh):
    fine = Mesh(mesh.devices.reshape(4, 2, 4, 2, 2), AXES)
    return jax.shard_map(
        local,
        mesh=fine,
        in_specs=(P(AXES, None),),
        out_specs=P(AXES, None),
        check_vma=False,
    )
```

```python
import jax
import jax.numpy as jnp
import numpy as np
from jax import lax
from jax.experimental import pallas as pl
from jax.experimental.pallas import tpu as pltpu
from jax.sharding import Mesh
from jax.sharding import PartitionSpec as P

NODES = 16
HALF = 512
WIDE = 1024
TILE = 256
PER = 64
ROWS = NODES * PER
AXES = ("x", "zh", "y", "zl", "core")
NODE_AXES = ("x", "y")
F32 = jnp.float32
BF16 = jnp.bfloat16
VMEM = pl.BlockSpec(memory_space=pltpu.VMEM)
SMEM = pl.BlockSpec(memory_space=pltpu.SMEM)
HBM = pl.BlockSpec(memory_space=pl.ANY)

RING = [0] + list(range(1, 32, 2)) + list(range(30, 0, -2))


def node_places():
    places = []
    for x in range(4):
        places += [x * 4 + (y if x % 2 == 0 else 3 - y) for y in range(4)]
    return places


PLACE = node_places()
NODE_AT = [PLACE.index(n) for n in range(NODES)]


def edge_pair(edge):
    return 2 * edge if edge <= 15 else 63 - 2 * edge


def flat(place, z, core):
    x, y = divmod(place, 4)
    zh, zl = divmod(z, 2)
    return (((x * 2 + zh) * 4 + y) * 2 + zl) * 2 + core


def all_perm(target):
    return [
        (flat(PLACE[j], z, c), flat(*target(j, z, c)))
        for j in range(NODES)
        for z in range(4)
        for c in range(2)
    ]


CORE_SWAP = all_perm(lambda j, z, c: (PLACE[j], z, 1 - c))
Z_EVEN = all_perm(lambda j, z, c: (PLACE[j], z ^ 1, c))
Z_ODD = all_perm(lambda j, z, c: (PLACE[j], 3 - z, c))
RING_BACK = all_perm(lambda j, z, c: (PLACE[(j - 1) % NODES], z, c))


def permute(value, table):
    return lax.ppermute(value, AXES, table)


def params(mebibytes=40):
    return pltpu.CompilerParams(vmem_limit_bytes=mebibytes * 1024 * 1024)


def cost(macs, nbytes):
    return pl.CostEstimate(flops=2 * macs, bytes_accessed=nbytes, transcendentals=0)


def struct(shape, dtype):
    return jax.ShapeDtypeStruct(shape, dtype)


def gram_dot(left, right):
    return lax.dot_general(left, right, (((0,), (0,)), ((), ())), preferred_element_type=F32)


GROUP = 4


def spread_kernel(weight_ref, *refs):
    outs, (held, load_sems, store_sems) = refs[:2], refs[2:]
    loads, stores = [], []
    for first, out_ref in enumerate(outs):
        for n in range(NODES):
            pair, place = RING[2 * NODE_AT[n] + first], first * NODES + n
            columns = weight_ref.at[:, pl.ds(pair * WIDE, WIDE)]
            loads.append(pltpu.make_async_copy(columns, held.at[place], load_sems.at[place]))
        for k in range(0, NODES, GROUP):
            place = first * NODES + k
            source, target = held.at[pl.ds(place, GROUP)], out_ref.at[pl.ds(k, GROUP)]
            stores.append(pltpu.make_async_copy(source, target, store_sems.at[place]))
    for load in loads:
        load.start()
    for k, store in enumerate(stores):
        for load in loads[GROUP * k : GROUP * (k + 1)]:
            load.wait()
        store.start()
    for store in stores:
        store.wait()


def spread(weight):
    out = struct((NODES, PER, WIDE), BF16)
    return pl.pallas_call(
        spread_kernel,
        out_shape=(out, out),
        in_specs=[HBM],
        out_specs=(HBM, HBM),
        scratch_shapes=[
            pltpu.VMEM((2 * NODES, PER, WIDE), BF16),
            pltpu.SemaphoreType.DMA((2 * NODES,)),
            pltpu.SemaphoreType.DMA((2 * NODES,)),
        ],
        compiler_params=params(60),
        cost_estimate=cost(0, 4 * ROWS * WIDE * 2),
        name="spread",
    )(weight)


def gather(parts, first, whole, name):
    def kernel(parts_ref, *refs):
        out_ref, sems = refs[-2:]
        stores = []
        for n in range(NODES):
            pair = edge_pair(2 * NODE_AT[n] + first)
            columns = out_ref.at[:, pl.ds(pair * WIDE, WIDE)]
            stores.append(pltpu.make_async_copy(parts_ref.at[n], columns, sems.at[n]))
        for store in stores:
            store.start()
        for store in stores:
            store.wait()

    operands = (parts,) if whole is None else (parts, whole)
    return pl.pallas_call(
        kernel,
        out_shape=struct((PER, 2 * NODES * WIDE), BF16),
        in_specs=[VMEM, HBM][: len(operands)],
        out_specs=HBM,
        scratch_shapes=[pltpu.SemaphoreType.DMA((NODES,))],
        input_output_aliases={} if whole is None else {1: 0},
        compiler_params=params(),
        cost_estimate=cost(0, 2 * ROWS * WIDE * 2),
        name=name,
    )(*operands)


TILES = [(0, 0), (0, 1), (1, 1), (0, 2), (0, 3), (2, 2), (2, 3), (3, 3), (1, 2), (1, 3)]


def gram_body(core, first, second, mine_ref, other_ref):
    def put(row, col, tile):
        owner, slot = divmod(TILES.index((row, col)), 5)
        for half in range(2):
            part = tile[half * 128 : (half + 1) * 128]

            @pl.when(core == owner)
            def _():
                mine_ref[2 * slot + half] = part

            @pl.when(core != owner)
            def _():
                other_ref[2 * slot + half] = part.astype(BF16)

    for block, cols in ((0, first), (2, second)):
        for i in range(2):
            left = cols[:, i * TILE : (i + 1) * TILE]
            strip = gram_dot(left, cols[:, i * TILE :])
            for j in range(i, 2):
                put(block + i, block + j, strip[:, (j - i) * TILE : (j - i + 1) * TILE])
            if block == 0:
                strip = gram_dot(left, second[...])
                for j in range(2):
                    put(i, 2 + j, strip[:, j * TILE : (j + 1) * TILE])


def gram_whole_kernel(core_ref, cols_ref, after_ref, mine_ref, other_ref):
    first, second = cols_ref.at[:, pl.ds(0, HALF)], cols_ref.at[:, pl.ds(HALF, HALF)]
    gram_body(core_ref[0], first, second, mine_ref, other_ref)


def gram_halves_kernel(core_ref, first_ref, second_ref, after_ref, mine_ref, other_ref):
    gram_body(core_ref[0], first_ref, second_ref, mine_ref, other_ref)


def gram(core, cols, after, name):
    return pl.pallas_call(
        gram_whole_kernel if len(cols) == 1 else gram_halves_kernel,
        out_shape=(struct((10, 128, TILE), F32), struct((10, 128, TILE), BF16)),
        in_specs=[SMEM] + [VMEM] * len(cols) + [HBM],
        out_specs=(VMEM, VMEM),
        compiler_params=params(),
        cost_estimate=cost(10 * ROWS * TILE * TILE, ROWS * WIDE * 2 + 2**21),
        name=name,
    )(core, *cols, after)


def mixed_kernel(core_ref, done_ref, cols_ref, mine_ref, other_ref):
    for i in range(2):
        strip = gram_dot(done_ref[:, i * TILE : (i + 1) * TILE], cols_ref[...])
        for half in range(2):
            part = strip[half * 128 : (half + 1) * 128]

            @pl.when(core_ref[0] == i)
            def _():
                mine_ref[half] = part

            @pl.when(core_ref[0] != i)
            def _():
                other_ref[half] = part.astype(BF16)


def mixed(core, done, cols, name):
    return pl.pallas_call(
        mixed_kernel,
        out_shape=(struct((2, 128, WIDE), F32), struct((2, 128, WIDE), BF16)),
        in_specs=[SMEM, VMEM, VMEM],
        out_specs=(VMEM, VMEM),
        compiler_params=params(),
        cost_estimate=cost(ROWS * HALF * WIDE, ROWS * WIDE * 3 + 2**21),
        name=name,
    )(core, done, cols)


def add(left, right):
    return (left.astype(F32) + right.astype(F32)).astype(BF16)


def first_add_kernel(mine, far, low_ref, high_ref):
    cut = low_ref.shape[0]
    low_ref[...] = (mine[:cut] + far[:cut].astype(F32)).astype(BF16)
    high_ref[...] = (mine[cut:] + far[cut:].astype(F32)).astype(BF16)


def first_add(mine, far):
    shape = struct((mine.shape[0] // 2,) + mine.shape[1:], BF16)
    return pl.pallas_call(
        first_add_kernel,
        out_shape=(shape, shape),
        in_specs=[VMEM] * 2,
        out_specs=(VMEM, VMEM),
        compiler_params=params(),
        cost_estimate=cost(0, 2**21),
        name="first_add",
    )(mine, far)


def total(mine, other):
    low, high = first_add(mine, permute(other, CORE_SWAP))
    midway, high = add(low, permute(low, Z_EVEN)), add(high, permute(high, Z_ODD))
    low, high = add(midway, permute(midway, Z_ODD)), add(high, permute(high, Z_EVEN))
    return (low, high, permute(low, CORE_SWAP), permute(high, CORE_SWAP)), midway


def rotation_body(tiles, sign, slot, rot_ref, gen, gen_low, middle):
    rows = lax.broadcasted_iota(jnp.int32, (TILE, TILE), 0)
    cols = lax.broadcasted_iota(jnp.int32, (TILE, TILE), 1)
    down, across = [], []
    for i in range(4):
        only = jnp.where(rows == cols, tiles(i, i), 0.0)
        down.append(jnp.sum(only, axis=1, keepdims=True))
        across.append(jnp.sum(only, axis=0, keepdims=True))
    total = jnp.zeros((TILE, TILE), F32)
    for i in range(4):
        for j in range(i, 4):
            upper = tiles(i, j) / (down[i] + across[j] + 0.001)
            if i == j:
                upper = jnp.where(rows < cols, upper, 0.0)
            elif i < 2 <= j:
                upper = upper * sign
            total = total + upper * upper
            at_i, at_j = pl.ds(i * TILE, TILE), pl.ds(j * TILE, TILE)
            if i == j:
                both = upper - upper.T
                gen[at_i, at_j] = both
                gen_low[at_i, at_j] = both.astype(BF16)
            else:
                flipped = -upper.T
                gen[at_i, at_j] = upper
                gen_low[at_i, at_j] = upper.astype(BF16)
                gen[at_j, at_i] = flipped
                gen_low[at_j, at_i] = flipped.astype(BF16)
    norm_sq = 1.0 + 2.0 * jnp.sum(total, keepdims=True) / WIDE
    inv_norm = lax.rsqrt(norm_sq)
    scale = 0.5 * inv_norm * inv_norm
    wide_rows = lax.broadcasted_iota(jnp.int32, (TILE, WIDE), 0)
    wide_cols = lax.broadcasted_iota(jnp.int32, (TILE, WIDE), 1)
    for i in range(4):
        at = pl.ds(i * TILE, TILE)
        squared = jnp.dot(gen_low[at, :], gen_low[...], preferred_element_type=F32)
        identity = jnp.where(wide_rows + i * TILE == wide_cols, 1.0, 0.0)
        middle[at, :] = (1.5 * identity - scale * (identity - squared)).astype(BF16)
    for i in range(4):
        at = pl.ds(i * TILE, TILE)
        identity = jnp.where(wide_rows + i * TILE == wide_cols, 1.0, 0.0)
        start_rot = ((identity + gen[at, :]) * inv_norm).astype(BF16)
        strip = jnp.dot(start_rot, middle[...], preferred_element_type=F32).astype(BF16)
        rot_ref[slot, at, :] = strip[:, :HALF]
        rot_ref[1 - slot, at, :] = strip[:, HALF:]


ROTATION_SCRATCH = [
    pltpu.VMEM((WIDE, WIDE), F32),
    pltpu.VMEM((WIDE, WIDE), BF16),
    pltpu.VMEM((WIDE, WIDE), BF16),
]


def hold(core, sums, held):
    own_low, own_high, far_low, far_high = sums
    cut = own_low.shape[0]
    held[core, :cut] = own_low[...]
    held[core, cut:] = own_high[...]
    held[1 - core, :cut] = far_low[...]
    held[1 - core, cut:] = far_high[...]


def held_tile(held, i, j):
    owner, slot = divmod(TILES.index((i, j)), 5)
    return held[owner, 2 * slot : 2 * slot + 2].reshape(TILE, TILE)


HELD = [pltpu.VMEM((2, 10, 128, TILE), BF16)]
DIAG = [(0, 0), (0, 1), (1, 1)]


def rotation_kernel(flags_ref, *refs):
    rot_ref, gen, gen_low, middle, held = refs[4:]
    hold(flags_ref[0], refs[:4], held)
    sign = jnp.where(flags_ref[1] == 1, 1.0, -1.0)

    def tiles(i, j):
        return held_tile(held, i, j).astype(F32)

    rotation_body(tiles, sign, 1 - flags_ref[1], rot_ref, gen, gen_low, middle)


def rotation(flags, sums, name):
    return pl.pallas_call(
        rotation_kernel,
        out_shape=struct((2, WIDE, HALF), BF16),
        in_specs=[SMEM] + [VMEM] * 4,
        out_specs=VMEM,
        scratch_shapes=ROTATION_SCRATCH + HELD,
        compiler_params=params(),
        cost_estimate=cost(2 * WIDE**3, 4 * 2**20),
        name=name,
    )(flags, *sums)


def rotation_diag_kernel(flags_ref, *refs):
    rot_ref, diag_ref, gen, gen_low, middle, held, gram_all, turned = refs[4:]
    hold(flags_ref[0], refs[:4], held)

    def tiles(i, j):
        return held_tile(held, i, j).astype(F32)

    rotation_body(tiles, 1.0, 0, rot_ref, gen, gen_low, middle)
    for i in range(4):
        for j in range(i, 4):
            at_i, at_j = pl.ds(i * TILE, TILE), pl.ds(j * TILE, TILE)
            tile = held_tile(held, i, j)
            gram_all[at_i, at_j] = tile
            if i != j:
                gram_all[at_j, at_i] = tile.astype(F32).T.astype(BF16)
    rot = rot_ref.at[flags_ref[2]]
    for i in range(4):
        at = pl.ds(i * TILE, TILE)
        turned[at, :] = jnp.dot(gram_all[at, :], rot[...], preferred_element_type=F32).astype(BF16)
    for place, (i, j) in enumerate(DIAG):
        at_i, at_j = pl.ds(i * TILE, TILE), pl.ds(j * TILE, TILE)
        diag_ref[place] = gram_dot(rot[:, at_i], turned[:, at_j])


def rotation_diag(flags, sums, name):
    return pl.pallas_call(
        rotation_diag_kernel,
        out_shape=(struct((2, WIDE, HALF), BF16), struct((3, TILE, TILE), F32)),
        in_specs=[SMEM] + [VMEM] * 4,
        out_specs=(VMEM, VMEM),
        scratch_shapes=ROTATION_SCRATCH
        + HELD
        + [pltpu.VMEM((WIDE, WIDE), BF16), pltpu.VMEM((WIDE, HALF), BF16)],
        compiler_params=params(),
        cost_estimate=cost(3 * WIDE**3, 6 * 2**20),
        name=name,
    )(flags, *sums)


def rotation_mixed_kernel(flags_ref, rot_b, diag_a, diag_b, *refs):
    rot_ref, gen, gen_low, middle, held, cross = refs[4:]
    hold(flags_ref[0], refs[:4], held)
    sign = jnp.where(flags_ref[1] == 1, 1.0, -1.0)
    for i in range(2):
        strip = held[i].reshape(TILE, WIDE)
        cross[i] = jnp.dot(strip, rot_b[flags_ref[2]], preferred_element_type=F32)

    def tiles(i, j):
        if i < 2 <= j:
            return cross[i, :, (j - 2) * TILE : (j - 1) * TILE]
        if j < 2:
            return diag_a[DIAG.index((i, j))]
        return diag_b[DIAG.index((i - 2, j - 2))]

    rotation_body(tiles, sign, 1 - flags_ref[1], rot_ref, gen, gen_low, middle)


def rotation_mixed(flags, rot_b, diag_a, diag_b, sums, name):
    return pl.pallas_call(
        rotation_mixed_kernel,
        out_shape=struct((2, WIDE, HALF), BF16),
        in_specs=[SMEM] + [VMEM] * 7,
        out_specs=VMEM,
        scratch_shapes=ROTATION_SCRATCH
        + [pltpu.VMEM((2, 2, 128, WIDE), BF16), pltpu.VMEM((2, TILE, HALF), F32)],
        compiler_params=params(),
        cost_estimate=cost(2 * WIDE**3 + WIDE**3 // 4, 6 * 2**20),
        name=name,
    )(flags, rot_b, diag_a, diag_b, *sums)


CHUNK = 256


def half_kernel(half_ref, cols_ref, rot_ref, out_ref):
    half = half_ref[0]
    for k in range(ROWS // CHUNK):
        at = pl.ds(k * CHUNK, CHUNK)
        out = jnp.dot(cols_ref[at, :], rot_ref[half], preferred_element_type=F32)
        out_ref[at, :] = out.astype(BF16)


def apply_half(half, cols, rot, name):
    return pl.pallas_call(
        half_kernel,
        out_shape=struct((ROWS, HALF), BF16),
        in_specs=[SMEM, VMEM, VMEM],
        out_specs=VMEM,
        compiler_params=params(),
        cost_estimate=cost(ROWS * WIDE * HALF, ROWS * WIDE * 3 + 2**20),
        name=name,
    )(half, cols, rot)


def both_kernel(first_ref, second_ref, rot_ref, out_ref):
    for k in range(ROWS // CHUNK):
        at = pl.ds(k * CHUNK, CHUNK)
        cols = jnp.concatenate([first_ref[at, :], second_ref[at, :]], axis=1)
        for half in range(2):
            out = jnp.dot(cols, rot_ref[half], preferred_element_type=F32)
            out_ref[at, half * HALF : (half + 1) * HALF] = out.astype(BF16)


def apply_both(first, second, rot, name):
    return pl.pallas_call(
        both_kernel,
        out_shape=struct((ROWS, WIDE), BF16),
        in_specs=[VMEM] * 3,
        out_specs=VMEM,
        compiler_params=params(),
        cost_estimate=cost(ROWS * WIDE * WIDE, 2 * ROWS * WIDE * 2 + 2**21),
        name=name,
    )(first, second, rot)


def exchange(parts):
    return lax.all_to_all(parts, NODE_AXES, 0, 0, tiled=True)


def local(weight):
    core = lax.axis_index("core").astype(jnp.int32)
    node = jnp.asarray(np.array(NODE_AT, np.int32))[lax.axis_index(NODE_AXES)]
    core1 = core[None]

    def flags(first_is_upper, half=0):
        return jnp.stack([core, jnp.asarray(first_is_upper, jnp.int32), jnp.asarray(half, jnp.int32)])

    half_a = jnp.where(2 * node <= 16, 0, 1).astype(jnp.int32)
    half_b = jnp.where(2 * node + 1 <= 16, 1, 0).astype(jnp.int32)

    sent_a, sent_b = spread(weight)
    cols_a = exchange(sent_a).reshape(ROWS, WIDE)
    cols_b = exchange(sent_b).reshape(ROWS, WIDE)
    sums, _ = total(*gram(core1, (cols_a,), cols_a, "gram_a"))
    rot_a, diag_a = rotation_diag(flags(1, half_a), sums, "rotation_a")
    prev_a = apply_half(1 - half_a[None], cols_a, rot_a, "apply_a_prev")
    far_a = permute(prev_a, RING_BACK)
    in_a = apply_half(half_a[None], cols_a, rot_a, "apply_a_in")

    sums_b, _ = total(*gram(core1, (cols_b,), sums[1], "gram_b"))
    sums_mixed, midway = total(*mixed(core1, in_a, cols_b, "mixed"))
    rot_b, diag_b = rotation_diag(flags(1, half_b), sums_b, "rotation_b")
    in_b = apply_half(half_b[None], cols_b, rot_b, "apply_b_in")
    next_b = apply_half(1 - half_b[None], cols_b, rot_b, "apply_b_next")

    rot = rotation_mixed(
        flags(2 * node <= 15, half_b), rot_b, diag_a, diag_b, sums_mixed, "rotation_in"
    )
    parts = apply_both(in_a, in_b, rot, "apply_in").reshape(NODES, PER, WIDE)
    parts_in = exchange(parts)

    sums, _ = total(*gram(core1, (next_b, far_a), rot, "gram_off"))
    rot = rotation(flags(2 * node + 1 <= 15), sums, "rotation_off")
    parts = apply_both(next_b, far_a, rot, "apply_off").reshape(NODES, PER, WIDE)
    parts_off = exchange(parts)

    return gather(parts_off, 1, gather(parts_in, 0, None, "gather_in"), "gather_off")


def solution(mesh):
    fine = Mesh(mesh.devices.reshape(4, 2, 4, 2, 2), AXES)
    return jax.shard_map(
        local,
        mesh=fine,
        in_specs=(P(AXES, None),),
        out_specs=P(AXES, None),
        check_vma=False,
    )
```
